128 devices in a mesh: boxes: 128 (over y, z, x, core).
Axes of the slice: x: 4, y: 4, z: 4, core: 2. Of those that a mesh axis runs over, the one named last changes fastest.
Arguments:
- tile_mass: float32 [16384, 128], P('boxes'), may hold values from 0.5 to 2
- tile_frac: float32 [16384, 3, 128], P('boxes'), may hold values from 0 to 1
- tile_cell: int32 [16384, 128], P('boxes'), may hold values from 0 to 32767
- tile_level: int32 [16384, 128], P('boxes'), may hold values from 0 to 1
- tile_owner: int32 [16384, 1], P('boxes'), may hold values from 0 to 127; in each aligned block of 128 rows (0 to 127, 128 to 255, ...) at most 2 rows name the same one
- tile_count: int32 [128], P('boxes'), may hold values from 96 to 128, as said below
- box_owner: int32 [2, 128], replicated, may hold values from 0 to 127, each once within a row
- force_field: bfloat16 [2, 3, 4096, 1024], P(None, None, 'boxes'), may hold values from -6 to 6
Outputs:
- density: float32 [2, 4096, 1024], P(None, 'boxes')
- kick: float32 [16384, 3, 128], P('boxes')
The draws below stay inside these ranges and needn't reach their ends.
Inputs may be any that keep to these rules, and one draw needn't show every extreme that they name: `tile_owner`: among the tiles of one device no owner is named by more than 2 tiles, a bound that some block reaches. The first tile_count tiles of a device are live, the rest are padding; some device has all 128 live. `box_owner`: each row is a permutation: every device holds exactly one box of each level. `tile_cell`: x * 32 * 32 + y * 32 + z for the cell (x, y, z) of the box.
All inputs are finite; a program needn't handle non-finite values.
Results may differ from the reference program's by a relative error of at most 0.0031.
Values may be sent and summed in bfloat16 or wider, within the bound.
A program may use at most 128 MiB of HBM per device.

```python
import math
import jax
import jax.numpy as jnp
import numpy as np
from jax import lax

LEVELS = 2
BOX = 32
TILE = 128
LAT_X = 4
LAT_Z = 4
TILES_DEV = 128
CAP = 2
TILES = 16384
N_BOXES = 128


def draw_tile_count(key, part):
    key = jax.random.fold_in(key, 11)
    first_key, second_key = jax.random.split(key)
    counts = jax.random.randint(first_key, (N_BOXES,), max(1, 3 * TILES_DEV // 4), TILES_DEV + 1)
    fullest = jax.random.randint(second_key, (), 0, N_BOXES)
    return counts.at[fullest].set(TILES_DEV).astype(jnp.int32)


def set_ends(entries, rng, smallest, high):
    index_at = [jax.random.randint(jax.random.fold_in(rng, axis), (), 0, length) for axis, length in enumerate(entries.shape)]
    widest = entries.shape.index(max(entries.shape))
    next_to = index_at[:widest] + [(index_at[widest] + 1) % entries.shape[widest]] + index_at[widest + 1:]
    return entries.at[tuple(index_at)].set(smallest).at[tuple(next_to)].set(high)


def steps_of(rng, extent, cuts, smallest, high):
    level, own = 1.0, jax.random.fold_in(rng, 6)
    for dim, parts in cuts:
        heights = jnp.exp(jax.random.uniform(jax.random.fold_in(own, dim), (parts,), jnp.float32, smallest / len(cuts), high / len(cuts)))
        level = level * jnp.repeat(heights, extent[dim] // parts).reshape([-1 if axis == dim else 1 for axis in range(len(extent))])
    return level


def assign_block(key, own, number, rows, count, top, most, skew):
    order = jax.random.permutation(key, count)
    packed, ordinary = shares(count, rows * top, most, skew, True), shares(count, rows * top, most, skew, False)
    places = jnp.arange(count)

    def named(lengths, offset_by):
        used = int((lengths > 0).sum())
        fixed = max(1, used // 4)
        moved = fixed + (places - fixed + offset_by * (used - fixed)) % max(1, count - fixed)
        return jnp.zeros((count,), jnp.int32).at[order[jnp.where(places < fixed, places, moved)]].set(jnp.asarray(lengths, jnp.int32))

    lengths = jnp.where(number % 4 == 0, named(packed, number // 4), named(ordinary, number - number // 4 - 1))
    mixed = jax.random.permutation(jax.random.fold_in(own, 3), count)
    source_of, sink = mixed[0:count // 2 * 2:2], mixed[1:count // 2 * 2:2]
    margin = jnp.minimum(lengths[source_of] - 1, most - lengths[sink]) // 2
    margin = jnp.where((source_of == order[0]) | (sink == order[0]) | (lengths[sink] == 0), 0, jnp.maximum(margin, 0))
    moved = jax.random.randint(jax.random.fold_in(own, 4), (count // 2,), 0, 1 << 20) % (margin + 1)
    lengths = lengths.at[source_of].add(-moved).at[sink].add(moved)
    members = jnp.searchsorted(jnp.cumsum(lengths), jnp.arange(rows * top), side="right").astype(jnp.int32)
    table = members.reshape(top, rows).T
    table = table[jax.random.permutation(jax.random.fold_in(own, 1), rows)]
    offset_by = jax.random.randint(jax.random.fold_in(own, 2), (rows, 1), 0, top)
    return jnp.take_along_axis(table, (jnp.arange(top)[None, :] + offset_by) % top, axis=1)


def shares(number_of, total, limit, slope, full):
    weights = [(1 << 20) // math.isqrt(grade ** slope) + 1 for grade in range(1, number_of + 1)]
    largest = limit if full else min(limit, max(-(-total // number_of), total * weights[0] // sum(weights)))
    least = 1 if total - largest >= number_of - 1 else 0
    holding, surplus = [largest] + [least] * (number_of - 1), total - largest - least * (number_of - 1)
    while surplus > 0:
        movable = [i for i in range(1, number_of) if holding[i] < largest] or [i for i in range(1, number_of) if holding[i] < limit]
        whole, remaining = sum([weights[i] for i in movable]), surplus
        for i in movable:
            addition = min(limit - holding[i], max(1, remaining * weights[i] // whole), surplus)
            holding[i] = holding[i] + addition
            surplus = surplus - addition
    return np.array(holding)


def normal_values(rng, dims, scale, most, pieces=(), kind=jnp.bfloat16):
    array = scale * jax.random.normal(rng, dims, jnp.float32)
    if pieces:
        array = array * steps_of(rng, dims, pieces, -0.22, 0.18)
    return jnp.clip(array, -most, most).astype(kind)


def setup_inputs(seed: int = 0) -> dict:
    arg_keys = jax.random.split(jax.random.key(seed), 9)
    tile_mass = jnp.clip(jnp.exp(math.log(2.0) - 1.3862944 * jax.random.uniform(arg_keys[0], (TILES, TILE), jnp.float32) ** steps_of(arg_keys[0], (TILES, TILE), ((0, 128),), -0.2, 0.2)), 0.5, 2.0)
    tile_frac = jnp.clip(1.0 * jax.random.uniform(arg_keys[1], (TILES, 3, TILE), jnp.float32) ** steps_of(arg_keys[1], (TILES, 3, TILE), ((0, 128),), -0.2, 0.2), 0.0, 1.0)
    tile_cell = set_ends(jax.random.randint(arg_keys[2], (TILES, TILE), 0, BOX * BOX * BOX), jax.random.fold_in(arg_keys[2], 1), 0, (BOX * BOX * BOX) - 1).astype(jnp.int32)
    tile_level = set_ends(jax.random.randint(arg_keys[3], (TILES, TILE), 0, LEVELS), jax.random.fold_in(arg_keys[3], 1), 0, LEVELS - 1).astype(jnp.int32)
    tile_owner_keys = jax.random.split(jax.random.fold_in(arg_keys[4], 1), TILES // TILES_DEV)
    tile_owner_turns = jax.random.permutation(jax.random.fold_in(arg_keys[4], 3), TILES // TILES_DEV)
    tile_owner = jax.vmap(lambda own, number: assign_block(jax.random.fold_in(arg_keys[4], 2), own, number, TILES_DEV, N_BOXES, 1, CAP, 2))(tile_owner_keys, tile_owner_turns).reshape((TILES, 1))
    tile_count = draw_tile_count(jax.random.fold_in(arg_keys[8], 71), 0)
    box_owner = jax.vmap(lambda own: jax.random.permutation(own, N_BOXES))(jax.random.split(arg_keys[6], LEVELS)).reshape((LEVELS, N_BOXES)).astype(jnp.int32)
    force_field = normal_values(arg_keys[7], (LEVELS, 3, N_BOXES * BOX, BOX * BOX), 1.0, 6.0, ((2, 128),))
    return {"tile_mass": tile_mass, "tile_frac": tile_frac, "tile_cell": tile_cell, "tile_level": tile_level, "tile_owner": tile_owner, "tile_count": tile_count, "box_owner": box_owner, "force_field": force_field}


def corner_weights(coord):
    floored = jnp.floor(coord)
    weight = coord - floored
    return floored.astype(jnp.int32), 1.0 - weight, weight


def to_bfloat(values):
    rounded = lax.optimization_barrier(values.astype(jnp.bfloat16))
    return rounded.astype(jnp.float32)


def reference(tile_mass, tile_frac, tile_cell, tile_level, tile_owner, tile_count, box_owner, force_field):
    lat_y = N_BOXES // 16
    side = BOX
    tile_ids = jnp.arange(TILES, dtype=jnp.int32)
    live_tile = (tile_ids % TILES_DEV) < tile_count[tile_ids // TILES_DEV]
    places = jnp.arange(N_BOXES, dtype=jnp.int32)
    level_rows = jnp.arange(LEVELS, dtype=jnp.int32)[:, None]
    holder = jnp.zeros((LEVELS, N_BOXES), jnp.int32).at[level_rows, box_owner].set(
        jnp.broadcast_to(places[None, :], (LEVELS, N_BOXES)))
    owner_id = jnp.broadcast_to(tile_owner[:, 0:1], (TILES, TILE))
    held_box = holder[tile_level, owner_id]
    box_place = [held_box // (lat_y * LAT_Z), (held_box // LAT_Z) % lat_y, held_box % LAT_Z]
    digits = [tile_cell // (side * side), (tile_cell // side) % side, tile_cell % side]
    extents = [LAT_X * side, lat_y * side, LAT_Z * side]
    cells = []
    weights = []
    for axis_id in range(3):
        position = digits[axis_id].astype(jnp.float32) + tile_frac[:, axis_id, :]
        floored, low_weight, high_weight = corner_weights(position)
        global_cell = box_place[axis_id] * side + floored
        cells.append([global_cell % extents[axis_id], (global_cell + 1) % extents[axis_id]])
        weights.append([low_weight, high_weight])
    live_mass = jnp.where(live_tile[:, None], tile_mass, 0.0)
    densities = []
    kicks = jnp.zeros((TILES, 3, TILE), jnp.float32)
    for level_id in range(LEVELS):
        level_mass = jnp.where(tile_level == level_id, live_mass, 0.0)
        chosen = jnp.where((tile_level == level_id) & live_tile[:, None], 1.0, 0.0)
        field = force_field[level_id].reshape(3, N_BOXES, side, side, side)
        field = jnp.take(field, box_owner[level_id], axis=1).astype(jnp.float32)
        field = field.reshape(3, LAT_X, lat_y, LAT_Z, side, side, side)
        field = field.transpose(0, 1, 4, 2, 5, 3, 6).reshape(3, extents[0], extents[1], extents[2])
        grid = jnp.zeros((extents[0], extents[1], extents[2]), jnp.float32)
        for corner_x in range(2):
            mass_term = to_bfloat(level_mass * weights[0][corner_x])
            for corner_y in range(2):
                for corner_z in range(2):
                    cross = to_bfloat(weights[1][corner_y] * weights[2][corner_z])
                    where_x = cells[0][corner_x]
                    where_y = cells[1][corner_y]
                    where_z = cells[2][corner_z]
                    grid = grid.at[where_x, where_y, where_z].add(mass_term * cross)
                    sample = field[:, where_x, where_y, where_z]
                    term = chosen * weights[0][corner_x] * cross
                    kicks = kicks + jnp.transpose(term[None, :, :] * sample, (1, 0, 2))
        blocks = grid.reshape(LAT_X, side, lat_y, side, LAT_Z, side).transpose(0, 2, 4, 1, 3, 5)
        blocks = blocks.reshape(N_BOXES, side, side, side)
        blocks = jnp.take(blocks, holder[level_id], axis=0)
        densities.append(blocks.reshape(N_BOXES * side, side * side))
    return jnp.stack(densities), kicks
```

```python
import functools

import jax
import jax.numpy as jnp
import numpy as np
from jax import lax
from jax.experimental import pallas as pl
from jax.experimental.pallas import tpu as pltpu
from jax.sharding import PartitionSpec as P

MESH = pl.DeviceIdType.MESH
HIGHEST = lax.Precision.HIGHEST
LAT_X = 4
LAT_Z = 4
SIDE = 32
CELLS = SIDE * SIDE
WIDE = CELLS + 128
INNER = 8
GROUP = 4

direction_table = np.array(
    [[1, 0, 0], [0, 1, 0], [0, 0, 1], [1, 1, 0], [1, 0, 1], [0, 1, 1], [1, 1, 1]], dtype=np.int32
)


def iota(shape, dim):
    return lax.broadcasted_iota(jnp.int32, shape, dim)


def rim_sources(box_owner):
    levels, devices = box_owner.shape
    lat_y = devices // 16
    places = jnp.arange(devices, dtype=jnp.int32)
    holder = jnp.sum(
        jnp.where(box_owner[:, None, :] == places[None, :, None], places[None, None, :], 0), axis=2
    )
    coords = jnp.stack([holder // (lat_y * LAT_Z), holder // LAT_Z % lat_y, holder % LAT_Z])
    extents = jnp.asarray([LAT_X, lat_y, LAT_Z], dtype=jnp.int32)[:, None, None, None]
    steps = jnp.asarray(direction_table.T)[:, None, :, None]
    ways = []
    for sign in (1, -1):
        near = (coords[:, :, None, :] + sign * steps + extents) % extents
        box = (near[0] * lat_y + near[1]) * LAT_Z + near[2]
        ways.append(
            jnp.sum(
                jnp.where(box[..., None] == places, box_owner[:, None, None, :], 0), axis=3
            ).reshape(levels * 7, devices)
        )
    return ways


def kind_of(lane):
    kind = jnp.where(lane < 32, 1, jnp.where(lane < 64, 2, -1))
    kind = jnp.where(lane == 64, 5, jnp.where(lane == 65, 3, kind))
    kind = jnp.where(lane == 66, 4, jnp.where(lane == 67, 6, kind))
    return jnp.where(lane >= 96, 0, kind)


def fold_target(lane):
    target = jnp.where(lane < CELLS, 96 + lane % SIDE, -1)
    target = jnp.where((lane >= CELLS) & (lane < CELLS + 32), 65, target)
    target = jnp.where((lane >= CELLS + 32) & (lane < CELLS + 64), 66, target)
    return jnp.where(lane == CELLS + 64, 67, target)


def fold_row(lane):
    row = jnp.where(lane < CELLS, lane // SIDE, -1)
    row = jnp.where((lane >= CELLS) & (lane < CELLS + 32), lane - CELLS, row)
    row = jnp.where((lane >= CELLS + 32) & (lane < CELLS + 64), lane - CELLS - 32, row)
    return jnp.where(lane == CELLS + 64, 0, row)


def fold(rows, dtype, precision):
    amount = rows.shape[0]
    shape = (SIDE, WIDE)
    own = fold_row(iota(shape, 1)) == iota(shape, 0)
    parts = [jnp.where(own, rows[place : place + 1, :], 0.0) for place in range(amount)]
    picked = jnp.concatenate(parts, axis=0).astype(dtype)
    target = fold_target(iota((WIDE, 128), 0)) == iota((WIDE, 128), 1)
    pick = jnp.where(target, 1.0, 0.0).astype(dtype)
    return jnp.dot(picked, pick, preferred_element_type=jnp.float32, precision=precision)


def unfold(table, dtype, precision):
    target = fold_target(iota((128, WIDE), 1)) == iota((128, WIDE), 0)
    pick = jnp.where(target, 1.0, 0.0).astype(dtype)
    spread = jnp.dot(table, pick, preferred_element_type=jnp.float32, precision=precision)
    shape = (SIDE, WIDE)
    own = fold_row(iota(shape, 1)) == iota(shape, 0)
    rows = []
    for place in range(table.shape[0] // SIDE):
        part = jnp.where(own, spread[place * SIDE : (place + 1) * SIDE, :], 0.0)
        rows.append(jnp.sum(part, axis=0, keepdims=True))
    return rows


def plane_pick(dtype, flip):
    shape = (128, CELLS) if flip else (CELLS, 128)
    lane = iota(shape, 0 if flip else 1)
    cell = iota(shape, 1 if flip else 0)
    wanted = jnp.where(lane < 32, lane, jnp.where(lane < 64, (lane - 32) * SIDE, -1))
    wanted = jnp.where(lane == 64, 0, wanted)
    return jnp.where(cell == wanted, 1.0, 0.0).astype(dtype)


def slot_picks(owner_ref, count, devices, by_slot):
    tiles = owner_ref.shape[1]
    across = jnp.broadcast_to(owner_ref[...], (tiles, tiles))
    down = jnp.transpose(across)
    same = across == down
    first, second = iota((tiles, tiles), 0), iota((tiles, tiles), 1)
    picks = []
    if by_slot:
        earlier = jnp.where(same & (first < second), 1.0, 0.0)
        rank = jnp.sum(earlier, axis=0, keepdims=True)
        fits = (across == first) & (second < count)
    else:
        earlier = jnp.where(same & (second < first), 1.0, 0.0)
        rank = jnp.sum(earlier, axis=1, keepdims=True)
        fits = (down == second) & (first < count)
    for order in range(2):
        picks.append(jnp.where(fits & (rank == float(order)), 1.0, 0.0))
    return picks


def greet(devices, me):
    barrier = pltpu.get_barrier_semaphore()

    def signal(step, carry):
        peer = lax.rem(me + step, devices)
        pl.semaphore_signal(barrier, inc=1, device_id=(peer,), device_id_type=MESH)
        return carry

    lax.fori_loop(1, devices, signal, 0)
    return barrier


def block_copy(source, target, send, recv, devices, me, step):
    peer = lax.rem(me + step, devices)
    return pltpu.make_async_remote_copy(
        src_ref=source.at[pl.ds(pl.multiple_of(peer * 8, 8), 8)],
        dst_ref=target.at[pl.ds(pl.multiple_of(me * 8, 8), 8)],
        send_sem=send.at[step - 1],
        recv_sem=recv.at[step - 1],
        device_id=(peer,),
        device_id_type=MESH,
    )


def inner_copy(gathered, send, recv, me, step):
    place = lax.rem(me, INNER)
    peer = me - place + lax.rem(place + step, INNER)
    return pltpu.make_async_remote_copy(
        src_ref=gathered.at[place],
        dst_ref=gathered.at[place],
        send_sem=send.at[step - 1],
        recv_sem=recv.at[step - 1],
        device_id=(peer,),
        device_id_type=MESH,
    )


def outer_copy(leaving, arrived, send, recv, devices, me, step):
    outer = devices // INNER
    row = me // INNER
    other = lax.rem(row + step, outer)
    return pltpu.make_async_remote_copy(
        src_ref=leaving.at[other],
        dst_ref=arrived.at[row],
        send_sem=send.at[step - 1],
        recv_sem=recv.at[step - 1],
        device_id=(other * INNER + lax.rem(me, INNER),),
        device_id_type=MESH,
    )


def each(count, act):
    def body(step, carry):
        act(step)
        return carry

    lax.fori_loop(1, count, body, 0)


def choose(tables, place_of, level, depth, dtype):
    lane = iota((1, 128), 1)
    kind = kind_of(lane)
    total = None
    for direction in range(7):
        keep = jnp.where(kind == direction, 1.0, 0.0).astype(dtype)
        block = tables[place_of(direction), level * depth : (level + 1) * depth, :]
        part = block * keep
        total = part if total is None else total + part
    return total


def relay(sources, gathered, leaving, arrived, devices, levels, depth, me, dtype):
    place, row = lax.rem(me, INNER), me // INNER

    def body(other, carry):
        target = other * INNER + place
        for level in range(levels):

            def place_of(direction):
                return lax.rem(sources[level * 7 + direction, target], INNER)

            leaving[other, level * depth : (level + 1) * depth, :] = choose(
                gathered, place_of, level, depth, dtype
            )
        return carry

    lax.fori_loop(0, devices // INNER, body, 0)
    arrived[row] = leaving[row]


def final_table(sources, arrived, level, depth, me, dtype):
    def row_of(direction):
        return sources[level * 7 + direction, me] // INNER

    return choose(arrived, row_of, level, depth, dtype)


def ship_kernel(
    devices,
    levels,
    sources,
    count_ref,
    owner_ref,
    mass_ref,
    frac_ref,
    cell_ref,
    level_ref,
    force_ref,
    inbox,
    rims,
    outbox,
    gathered,
    leaving,
    arrived,
    self_sem,
    tile_send,
    tile_recv,
    inner_send,
    inner_recv,
    outer_send,
    outer_recv,
):
    me = lax.axis_index("boxes")
    depth = 3 * SIDE
    bf16 = jnp.bfloat16
    barrier = greet(devices, me)
    force = force_ref[...]
    near = jnp.dot(force, plane_pick(bf16, False), preferred_element_type=jnp.float32)
    wide = []
    for place in range(levels * 3):
        at = place * SIDE
        front = force_ref[at : at + 16, :].astype(jnp.float32)[0:1, :]
        wide.append(jnp.concatenate([front, near[at : at + 1, :]], axis=1))
    table = near + fold(jnp.concatenate(wide, axis=0), bf16, None)
    gathered[lax.rem(me, INNER)] = table.astype(bf16)

    picks = slot_picks(owner_ref, count_ref[0], devices, True)
    cell = cell_ref[...]
    digits = [cell // CELLS, cell // SIDE % SIDE, cell % SIDE]
    fields = [jnp.where(level_ref[...] == 0, mass_ref[...], -mass_ref[...])]
    for axis in range(3):
        fields.append(digits[axis].astype(jnp.float32) + frac_ref[:, axis, :])
    for order in range(2):
        for place in range(4):
            moved = jnp.dot(
                picks[order], fields[place], preferred_element_type=jnp.float32, precision=HIGHEST
            )
            outbox[pl.ds(order * 4 + place, devices, stride=8), :] = moved

    pl.semaphore_wait(barrier, devices - 1)
    each(INNER, lambda step: inner_copy(gathered, inner_send, inner_recv, me, step).start())
    each(
        devices,
        lambda step: block_copy(outbox, inbox, tile_send, tile_recv, devices, me, step).start(),
    )
    own = pltpu.make_async_copy(
        outbox.at[pl.ds(pl.multiple_of(me * 8, 8), 8)],
        inbox.at[pl.ds(pl.multiple_of(me * 8, 8), 8)],
        self_sem,
    )
    own.start()
    each(INNER, lambda step: inner_copy(gathered, inner_send, inner_recv, me, step).wait())
    relay(sources, gathered, leaving, arrived, devices, levels, depth, me, bf16)
    outer = devices // INNER
    each(
        outer,
        lambda step: outer_copy(
            leaving, arrived, outer_send, outer_recv, devices, me, step
        ).start(),
    )
    each(
        outer,
        lambda step: outer_copy(leaving, arrived, outer_send, outer_recv, devices, me, step).wait(),
    )
    for level in range(levels):
        rims[level * depth : (level + 1) * depth, :] = final_table(
            sources, arrived, level, depth, me, bf16
        )
    own.wait()
    each(
        devices,
        lambda step: block_copy(outbox, inbox, tile_send, tile_recv, devices, me, step).wait(),
    )


def hat(coord, rows, start):
    ids = iota((rows, coord.shape[1]), 0).astype(jnp.float32) + start
    return jnp.maximum(0.0, 1.0 - jnp.abs(coord - ids))


def sweep_kernel(
    devices, levels, inbox, force_ref, rims, kicks, density, upper, table, cross, weighted, total
):
    bf16 = jnp.bfloat16
    rows = levels * 3 * SIDE
    depth = 3 * SIDE
    table[0:rows, 0:CELLS] = force_ref[...]
    table[0:rows, CELLS:WIDE] = rims[...]
    beyond = unfold(rims[...], bf16, None)
    beyond.append(jnp.zeros((16 - len(beyond), WIDE), jnp.float32))
    table[rows : rows + 16, :] = jnp.concatenate(beyond, axis=0).astype(bf16)
    cross[...] = jnp.zeros_like(cross)
    weighted[...] = jnp.zeros_like(weighted)
    total[...] = jnp.zeros_like(total)

    def advance(block, carry):
        info = []
        for part in range(GROUP):
            lanes = slice(part * 128, (part + 1) * 128)
            first = pl.multiple_of(block * (GROUP // 2 * 8), 8) + part * 4
            mass = inbox[pl.ds(first, 1), :]
            along = [inbox[pl.ds(first + 1 + axis, 1), :] for axis in range(3)]
            hat_x, hat_y, hat_z = [hat(along[axis], SIDE, 0.0) for axis in range(3)]
            end_x, end_y, end_z = [hat(along[axis], 1, float(SIDE)) for axis in range(3)]
            for y in range(SIDE):
                cross[y * SIDE : (y + 1) * SIDE, lanes] = (hat_y[y : y + 1, :] * hat_z).astype(bf16)
            cross[CELLS : CELLS + 32, lanes] = (end_y * hat_z).astype(bf16)
            cross[CELLS + 32 : CELLS + 64, lanes] = (hat_y * end_z).astype(bf16)
            last = jnp.where(iota((16, 128), 0) == 0, end_y * end_z, 0.0)
            cross[CELLS + 64 : CELLS + 80, lanes] = last.astype(bf16)
            for level in range(levels):
                own = jnp.maximum(mass if level == 0 else -mass, 0.0)
                weighted[level * SIDE : (level + 1) * SIDE, lanes] = (own * hat_x).astype(bf16)
            ends = jnp.where(iota((16, 128), 0) == 0, jnp.maximum(mass, 0.0), 0.0)
            ends = jnp.where(iota((16, 128), 0) == 1, jnp.maximum(-mass, 0.0), ends)
            weighted[2 * SIDE : 2 * SIDE + 16, lanes] = (ends * end_x).astype(bf16)
            info.append((first, mass, hat_x, end_x))
        total[...] += lax.dot_general(
            cross[...],
            weighted[...],
            (((1,), (1,)), ((), ())),
            preferred_element_type=jnp.float32,
        )
        sampled = jnp.dot(table[...], cross[...], preferred_element_type=jnp.float32)
        for part in range(GROUP):
            lanes = slice(part * 128, (part + 1) * 128)
            first, mass, hat_x, end_x = info[part]
            upper_level = mass < 0.0
            for axis in range(3):
                at = axis * SIDE
                picked = jnp.where(
                    upper_level,
                    sampled[depth + at : depth + at + SIDE, lanes],
                    sampled[at : at + SIDE, lanes],
                )
                far = jnp.where(
                    upper_level,
                    sampled[rows + 3 + axis : rows + 4 + axis, lanes],
                    sampled[rows + axis : rows + axis + 1, lanes],
                )
                value = jnp.sum(hat_x * picked, axis=0, keepdims=True) + end_x * far
                kicks[pl.ds(first + axis, 1), :] = value
            kicks[pl.ds(first + 3, 1), :] = jnp.zeros((1, 128), jnp.float32)
        return carry

    lax.fori_loop(0, 2 * devices // GROUP, advance, 0)
    flipped = jnp.transpose(total[...])
    density[...] = flipped[0 : levels * SIDE, 0:CELLS]
    wide = flipped[levels * SIDE : levels * SIDE + levels, :]
    upper[...] = jnp.where(
        iota((levels * SIDE, 128), 1) < 65, flipped[0 : levels * SIDE, CELLS:WIDE], 0.0
    ) + fold(wide, jnp.float32, HIGHEST)


def settle_kernel(
    devices,
    levels,
    sources,
    count_ref,
    owner_ref,
    kicks,
    density_in,
    upper,
    density,
    kick,
    returned,
    gathered,
    leaving,
    arrived,
    self_sem,
    tile_send,
    tile_recv,
    inner_send,
    inner_recv,
    outer_send,
    outer_recv,
):
    me = lax.axis_index("boxes")
    f32 = jnp.float32
    depth = SIDE
    barrier = greet(devices, me)
    gathered[lax.rem(me, INNER)] = upper[...]
    pl.semaphore_wait(barrier, devices - 1)
    each(INNER, lambda step: inner_copy(gathered, inner_send, inner_recv, me, step).start())
    each(
        devices,
        lambda step: block_copy(kicks, returned, tile_send, tile_recv, devices, me, step).start(),
    )
    own = pltpu.make_async_copy(
        kicks.at[pl.ds(pl.multiple_of(me * 8, 8), 8)],
        returned.at[pl.ds(pl.multiple_of(me * 8, 8), 8)],
        self_sem,
    )
    own.start()
    picks = slot_picks(owner_ref, count_ref[0], devices, False)
    each(INNER, lambda step: inner_copy(gathered, inner_send, inner_recv, me, step).wait())
    relay(sources, gathered, leaving, arrived, devices, levels, depth, me, f32)
    outer = devices // INNER
    each(
        outer,
        lambda step: outer_copy(
            leaving, arrived, outer_send, outer_recv, devices, me, step
        ).start(),
    )
    each(
        outer,
        lambda step: outer_copy(leaving, arrived, outer_send, outer_recv, devices, me, step).wait(),
    )
    table = jnp.concatenate(
        [final_table(sources, arrived, level, depth, me, f32) for level in range(levels)], axis=0
    )
    wide = unfold(table, f32, HIGHEST)
    first_row = iota((SIDE, 1), 0) == 0
    near = jnp.concatenate(
        [
            table[level * SIDE : (level + 1) * SIDE, :]
            + jnp.where(first_row, wide[level][:, CELLS:WIDE], 0.0)
            for level in range(levels)
        ],
        axis=0,
    )
    added = jnp.dot(near, plane_pick(f32, True), preferred_element_type=f32, precision=HIGHEST)
    for level in range(levels):
        at = slice(level * SIDE, (level + 1) * SIDE)
        density[at, :] = (
            density_in[at, :] + added[at, :] + jnp.where(first_row, wide[level][:, 0:CELLS], 0.0)
        )
    own.wait()
    each(
        devices,
        lambda step: block_copy(kicks, returned, tile_send, tile_recv, devices, me, step).wait(),
    )
    for axis in range(3):
        mine = None
        for order in range(2):
            part = jnp.dot(
                picks[order],
                returned[pl.ds(order * 4 + axis, devices, stride=8), :],
                preferred_element_type=f32,
                precision=HIGHEST,
            )
            mine = part if mine is None else mine + part
        kick[:, axis, :] = mine


def on_device(
    tile_mass, tile_frac, tile_cell, tile_level, tile_owner, tile_count, box_owner, force_field
):
    devices = lax.axis_size("boxes")
    levels = box_owner.shape[0]
    tiles, width = tile_mass.shape
    rows = levels * 3 * SIDE
    outer = devices // INNER
    f32, bf16 = jnp.float32, jnp.bfloat16
    shape = jax.ShapeDtypeStruct
    vmem = pl.BlockSpec(memory_space=pltpu.VMEM)
    smem = pl.BlockSpec(memory_space=pltpu.SMEM)
    hbm = pl.BlockSpec(memory_space=pl.ANY)
    dma = pltpu.SemaphoreType.DMA
    lower_from, upper_from = rim_sources(box_owner)
    owner_row = tile_owner.reshape(1, tiles)
    force = force_field.reshape(rows, CELLS)
    semaphores = [
        dma,
        dma((devices - 1,)),
        dma((devices - 1,)),
        dma((INNER - 1,)),
        dma((INNER - 1,)),
        dma((outer - 1,)),
        dma((outer - 1,)),
    ]
    inbox, rims = pl.pallas_call(
        functools.partial(ship_kernel, devices, levels),
        out_shape=(shape((devices * 8, width), f32), shape((rows, 128), bf16)),
        in_specs=[smem, smem] + [vmem] * 6,
        out_specs=(hbm, vmem),
        scratch_shapes=[
            pltpu.VMEM((devices * 8, width), f32),
            pltpu.VMEM((INNER, rows, 128), bf16),
            pltpu.VMEM((outer, rows, 128), bf16),
            pltpu.VMEM((outer, rows, 128), bf16),
        ]
        + semaphores,
        compiler_params=pltpu.CompilerParams(
            collective_id=0, has_side_effects=True, vmem_limit_bytes=40 << 20
        ),
        name="ship",
    )(lower_from, tile_count, owner_row, tile_mass, tile_frac, tile_cell, tile_level, force)
    kicks, density, upper = pl.pallas_call(
        functools.partial(sweep_kernel, devices, levels),
        out_shape=(
            shape((devices * 8, width), f32),
            shape((levels * SIDE, CELLS), f32),
            shape((levels * SIDE, 128), f32),
        ),
        in_specs=[vmem] * 3,
        out_specs=(vmem, vmem, vmem),
        scratch_shapes=[
            pltpu.VMEM((rows + 16, WIDE), bf16),
            pltpu.VMEM((WIDE, GROUP * 128), bf16),
            pltpu.VMEM((128, GROUP * 128), bf16),
            pltpu.VMEM((WIDE, 128), f32),
        ],
        compiler_params=pltpu.CompilerParams(vmem_limit_bytes=40 << 20),
        name="sweep",
    )(inbox, force, rims)
    density, kick = pl.pallas_call(
        functools.partial(settle_kernel, devices, levels),
        out_shape=(shape((levels * SIDE, CELLS), f32), shape((tiles, 3, width), f32)),
        in_specs=[smem, smem] + [vmem] * 4,
        out_specs=(vmem, vmem),
        scratch_shapes=[
            pltpu.VMEM((devices * 8, width), f32),
            pltpu.VMEM((INNER, levels * SIDE, 128), f32),
            pltpu.VMEM((outer, levels * SIDE, 128), f32),
            pltpu.VMEM((outer, levels * SIDE, 128), f32),
        ]
        + semaphores,
        compiler_params=pltpu.CompilerParams(
            collective_id=1, has_side_effects=True, vmem_limit_bytes=40 << 20
        ),
        name="settle",
    )(upper_from, tile_count, owner_row, kicks, density, upper)
    return (density.reshape(levels, SIDE, CELLS), kick)


def solution(mesh):
    in_specs = (
        P("boxes", None),
        P("boxes", None, None),
        P("boxes", None),
        P("boxes", None),
        P("boxes", None),
        P("boxes"),
        P(),
        P(None, None, "boxes", None),
    )
    out_specs = (P(None, "boxes", None), P("boxes", None, None))
    return jax.shard_map(
        on_device, mesh=mesh, in_specs=in_specs, out_specs=out_specs, check_vma=False
    )
```

```python
import functools

import jax
import jax.numpy as jnp
import numpy as np
from jax import lax
from jax.experimental import pallas as pl
from jax.experimental.pallas import tpu as pltpu
from jax.sharding import PartitionSpec as P

MESH = pl.DeviceIdType.MESH
HIGHEST = lax.Precision.HIGHEST
F32 = jnp.float32
BF16 = jnp.bfloat16
LAT_X = 4
LAT_Z = 4
SIDE = 32
CELLS = SIDE * SIDE
WIDE = CELLS + 128
INNER = 8
SOURCES = 4
GROUP = 2 * SOURCES
LANES = GROUP * 128
CHUNK = 11
CHUNKS = 3
SHORT = (CHUNK + 1) * SIDE
RELAY_AT = 3

direction_table = np.array(
    [[1, 0, 0], [0, 1, 0], [0, 0, 1], [1, 1, 0], [1, 0, 1], [0, 1, 1], [1, 1, 1]], dtype=np.int32
)


def iota(shape, dim):
    return lax.broadcasted_iota(jnp.int32, shape, dim)


def ones_at(mask, dtype):
    return jnp.where(mask, 1.0, 0.0).astype(dtype)


def kind_of(lane):
    kind = jnp.where(lane < 32, 1, jnp.where(lane < 64, 2, -1))
    kind = jnp.where(lane == 64, 5, jnp.where(lane == 65, 3, kind))
    kind = jnp.where(lane == 66, 4, jnp.where(lane == 67, 6, kind))
    return jnp.where(lane >= 96, 0, kind)


def fold_target(lane):
    target = jnp.where(lane < CELLS, 96 + lane % SIDE, -1)
    target = jnp.where((lane >= CELLS) & (lane < CELLS + 32), 65, target)
    target = jnp.where((lane >= CELLS + 32) & (lane < CELLS + 64), 66, target)
    return jnp.where(lane == CELLS + 64, 67, target)


def fold_row(lane):
    row = jnp.where(lane < CELLS, lane // SIDE, -1)
    row = jnp.where((lane >= CELLS) & (lane < CELLS + 32), lane - CELLS, row)
    row = jnp.where((lane >= CELLS + 32) & (lane < CELLS + 64), lane - CELLS - 32, row)
    return jnp.where(lane == CELLS + 64, 0, row)


def fold(rows, dtype, precision):
    amount = rows.shape[0]
    shape = (SIDE, WIDE)
    own = fold_row(iota(shape, 1)) == iota(shape, 0)
    parts = [jnp.where(own, rows[place : place + 1, :], 0.0) for place in range(amount)]
    picked = jnp.concatenate(parts, axis=0).astype(dtype)
    pick = ones_at(fold_target(iota((WIDE, 128), 0)) == iota((WIDE, 128), 1), dtype)
    return jnp.dot(picked, pick, preferred_element_type=F32, precision=precision)


def unfold(table, dtype, precision):
    pick = ones_at(fold_target(iota((128, WIDE), 1)) == iota((128, WIDE), 0), dtype)
    spread = jnp.dot(table, pick, preferred_element_type=F32, precision=precision)
    shape = (SIDE, WIDE)
    own = fold_row(iota(shape, 1)) == iota(shape, 0)
    rows = []
    for place in range(table.shape[0] // SIDE):
        part = jnp.where(own, spread[place * SIDE : (place + 1) * SIDE, :], 0.0)
        rows.append(jnp.sum(part, axis=0, keepdims=True))
    return rows


def plane_pick(dtype, flip):
    shape = (128, CELLS) if flip else (CELLS, 128)
    lane = iota(shape, 0 if flip else 1)
    cell = iota(shape, 1 if flip else 0)
    wanted = jnp.where(lane < 32, lane, jnp.where(lane < 64, (lane - 32) * SIDE, -1))
    wanted = jnp.where(lane == 64, 0, wanted)
    return ones_at(cell == wanted, dtype)


def slot_picks(owner_ref, count, by_slot):
    tiles = owner_ref.shape[1]
    across = jnp.broadcast_to(owner_ref[...], (tiles, tiles))
    down = jnp.transpose(across)
    same = across == down
    first, second = iota((tiles, tiles), 0), iota((tiles, tiles), 1)
    if by_slot:
        earlier = jnp.where(same & (first < second), 1.0, 0.0)
        rank = jnp.sum(earlier, axis=0, keepdims=True)
        fits = (across == first) & (second < count)
    else:
        earlier = jnp.where(same & (second < first), 1.0, 0.0)
        rank = jnp.sum(earlier, axis=1, keepdims=True)
        fits = (down == second) & (first < count)
    picks = [jnp.where(fits & (rank == float(order)), 1.0, 0.0) for order in range(2)]
    return jnp.concatenate(picks, axis=0 if by_slot else 1)


def rim_sources(box_owner, level, devices):
    lat_y = devices // (LAT_X * LAT_Z)
    square = (devices, devices)
    across = jnp.broadcast_to(box_owner[level : level + 1, :], square)
    down = jnp.transpose(across).astype(F32).astype(BF16)
    hot = ones_at(across == iota(square, 0), BF16)
    places = iota(square, 0).astype(F32).astype(BF16)
    box = jnp.dot(hot, places, preferred_element_type=F32).astype(jnp.int32)
    at = [box // (lat_y * LAT_Z), box // LAT_Z % lat_y, box % LAT_Z]
    kind = kind_of(iota(square, 1))
    found = []
    for sign in (1, -1):
        hots = []
        for step in direction_table:
            near = [
                (at[axis] + (sign * int(step[axis]) + extent)) % extent
                for axis, extent in enumerate((LAT_X, lat_y, LAT_Z))
            ]
            wanted = (near[0] * lat_y + near[1]) * LAT_Z + near[2]
            hots.append(ones_at(wanted == iota(square, 1), BF16))
        owners = jnp.dot(jnp.concatenate(hots, axis=0), down, preferred_element_type=F32)
        total = jnp.zeros(square, F32)
        for direction in range(7):
            part = owners[direction * devices : (direction + 1) * devices, :]
            total = jnp.where(kind == direction, part, total)
        found.append(total)
    return found


def each(count, act):
    def body(step, carry):
        act(step)
        return carry

    lax.fori_loop(1, count, body, 0)


def block_rows(device):
    return pl.ds(pl.multiple_of(device * 8, 8), 8)


def block_copy(source, target, send, recv, devices, me, step):
    peer = lax.rem(me + step, devices)
    return pltpu.make_async_remote_copy(
        src_ref=source.at[block_rows(peer)],
        dst_ref=target.at[block_rows(me)],
        send_sem=send,
        recv_sem=recv,
        device_id=(peer,),
        device_id_type=MESH,
    )


def back_copy(source, target, send, recv, devices, me, step):
    peer = lax.rem(me + devices - step, devices)
    return pltpu.make_async_remote_copy(
        src_ref=source.at[block_rows(peer)],
        dst_ref=target.at[block_rows(me)],
        send_sem=send,
        recv_sem=recv,
        device_id=(peer,),
        device_id_type=MESH,
    )


def all_blocks(source, target, send, recv, devices, me):
    rows = (devices - 1) * 8
    return pltpu.make_async_remote_copy(
        src_ref=source.at[pl.ds(0, rows)],
        dst_ref=target.at[pl.ds(0, rows)],
        send_sem=send,
        recv_sem=recv,
        device_id=(lax.rem(me + 1, devices),),
        device_id_type=MESH,
    )


def inner_copy(gathered, send, recv, me, step):
    place = lax.rem(me, INNER)
    peer = me - place + lax.rem(place + step, INNER)
    return pltpu.make_async_remote_copy(
        src_ref=gathered.at[place],
        dst_ref=gathered.at[place],
        send_sem=send.at[step - 1],
        recv_sem=recv.at[step - 1],
        device_id=(peer,),
        device_id_type=MESH,
    )


def outer_copy(leaving, arrived, send, recv, devices, me, step):
    outer = devices // INNER
    row = me // INNER
    other = lax.rem(row + step, outer)
    return pltpu.make_async_remote_copy(
        src_ref=leaving.at[other],
        dst_ref=arrived.at[row],
        send_sem=send.at[step - 1],
        recv_sem=recv.at[step - 1],
        device_id=(other * INNER + lax.rem(me, INNER),),
        device_id_type=MESH,
    )


def choose(tables, wanted, level, depth, dtype):
    total = None
    for place in range(tables.shape[0]):
        keep = ones_at(wanted == float(place), dtype)
        part = tables[place, level * depth : (level + 1) * depth, :] * keep
        total = part if total is None else total + part
    return total


def relay(near, first, gathered, leaving, arrived, outer, levels, depth, me, dtype):
    place, row = lax.rem(me, INNER), me // INNER

    def body(other, carry):
        for level in range(levels):
            wanted = near[first + level, pl.ds(other * INNER + place, 1), :]
            wanted = wanted - INNER * jnp.floor(wanted / INNER)
            leaving[other, level * depth : (level + 1) * depth, :] = choose(
                gathered, wanted, level, depth, dtype
            )
        return carry

    lax.fori_loop(0, outer, body, 0)
    arrived[row] = leaving[row]


def final_table(near, first, arrived, level, depth, me, dtype):
    wanted = jnp.floor(near[first + level, pl.ds(me, 1), :] / INNER)
    return choose(arrived, wanted, level, depth, dtype)


def hat(coord, rows, start):
    ids = iota((rows, coord.shape[1]), 0).astype(F32) + start
    return jnp.maximum(0.0, 1.0 - jnp.abs(coord - ids))


def group_sources(devices, me, block):
    return [lax.rem(me + devices - (block * SOURCES + 1 + part), devices) for part in range(SOURCES)]


def group_fields(inbox, sources):
    fields = []
    for field in range(4):
        rows = []
        for source in sources:
            for order in range(2):
                rows.append(inbox[pl.ds(source * 8 + (order * 4 + field), 1), :])
        fields.append(jnp.concatenate(rows, axis=1))
    return fields


def fill_deposit(fields, short, weighted):
    mass, x, y, z = fields
    chunk = jnp.where(y >= 2.0 * CHUNK, 2.0, jnp.where(y >= CHUNK, 1.0, 0.0))
    hat_y = hat(y - chunk * CHUNK, 16, 0.0)
    hat_z = hat(z, SIDE, 0.0)
    for row in range(CHUNK + 1):
        short[row * SIDE : (row + 1) * SIDE, :] = (hat_y[row : row + 1, :] * hat_z).astype(BF16)
    tops = jnp.where(iota((16, LANES), 0) <= CHUNK, hat_y * hat(z, 1, float(SIDE)), 0.0)
    short[SHORT : SHORT + 16, :] = tops.astype(BF16)
    hat_x = hat(x, SIDE, 0.0)
    for place in range(CHUNKS):
        for level in range(2):
            own = jnp.maximum(mass if level == 0 else -mass, 0.0)
            own = jnp.where(chunk == float(place), own, 0.0)
            at = (place * 2 + level) * SIDE
            weighted[at : at + SIDE, :] = (own * hat_x).astype(BF16)
    row_of = 2.0 * chunk + jnp.where(mass < 0.0, 1.0, 0.0)
    ends = jnp.where(iota((16, LANES), 0).astype(F32) == row_of, jnp.abs(mass), 0.0)
    at = CHUNKS * 2 * SIDE
    weighted[at : at + 16, :] = (ends * hat(x, 1, float(SIDE))).astype(BF16)


def add_deposit(short, weighted, total):
    product = lax.dot_general(
        short[...], weighted[...], (((1,), (1,)), ((), ())), preferred_element_type=F32
    )
    total[:, 0 : product.shape[1]] += product


def fill_cross(fields, cross):
    _, _, y, z = fields
    hat_y, hat_z = hat(y, SIDE, 0.0), hat(z, SIDE, 0.0)
    end_y, end_z = hat(y, 1, float(SIDE)), hat(z, 1, float(SIDE))
    for row in range(SIDE):
        cross[row * SIDE : (row + 1) * SIDE, :] = (hat_y[row : row + 1, :] * hat_z).astype(BF16)
    cross[CELLS : CELLS + 32, :] = (end_y * hat_z).astype(BF16)
    cross[CELLS + 32 : CELLS + 64, :] = (hat_y * end_z).astype(BF16)
    last = jnp.where(iota((16, LANES), 0) == 0, end_y * end_z, 0.0)
    cross[CELLS + 64 : CELLS + 80, :] = last.astype(BF16)


def sample(fields, sources, table, cross, kicks):
    mass, x, _, _ = fields
    rows = table.shape[0] - 16
    depth = rows // 2
    sampled = jnp.dot(table[...], cross[...], preferred_element_type=F32)
    hat_x, end_x = hat(x, SIDE, 0.0), hat(x, 1, float(SIDE))
    upper_level = mass < 0.0
    for axis in range(3):
        at = axis * SIDE
        picked = jnp.where(
            upper_level, sampled[depth + at : depth + at + SIDE, :], sampled[at : at + SIDE, :]
        )
        at = rows + axis
        far = jnp.where(upper_level, sampled[at + 3 : at + 4, :], sampled[at : at + 1, :])
        value = jnp.sum(hat_x * picked, axis=0, keepdims=True) + end_x * far
        for part, source in enumerate(sources):
            for order in range(2):
                lanes = slice((part * 2 + order) * 128, (part * 2 + order + 1) * 128)
                kicks[pl.ds(source * 8 + (order * 4 + axis), 1), :] = value[:, lanes]


def spread_deposit(total, wide):
    wide[...] = jnp.zeros_like(wide)
    first, second = total[:, 0:128], total[:, 128:256]
    low = iota(first.shape, 1) < 2 * SIDE
    for place in range(CHUNKS):
        main = [first, pltpu.roll(first, 64, 1), second][place]
        ends = second if place == 0 else pltpu.roll(second, 128 - 2 * place, 1)
        both = jnp.where(low, main, ends)
        at = place * CHUNK * SIDE
        wide[at : at + SHORT, :] += both[0:SHORT, :]
        at = CELLS + SIDE + place * CHUNK
        wide[at : at + CHUNK + 1, :] += both[SHORT : SHORT + CHUNK + 1, :]


def kernel(
    devices,
    levels,
    count_ref,
    owner_ref,
    box_owner,
    mass_ref,
    frac_ref,
    cell_ref,
    level_ref,
    force_ref,
    density,
    kick,
    outbox,
    inbox,
    kicks,
    returned,
    near,
    force_gathered,
    force_leaving,
    force_arrived,
    mass_gathered,
    mass_leaving,
    mass_arrived,
    table,
    cross_a,
    cross_b,
    short_a,
    short_b,
    weighted_a,
    weighted_b,
    total,
    wide,
    own_sem,
    tile_send,
    tile_recv,
    kick_send,
    kick_recv,
    inner_send,
    inner_recv,
    outer_send,
    outer_recv,
    inner_send2,
    inner_recv2,
    outer_send2,
    outer_recv2,
):
    me = lax.axis_index("boxes")
    outer = devices // INNER
    depth = 3 * SIDE
    rows = levels * depth
    groups = devices // SOURCES
    pairs = groups // 2

    barrier = pltpu.get_barrier_semaphore()
    each(
        devices,
        lambda step: pl.semaphore_signal(
            barrier, inc=1, device_id=(lax.rem(me + step, devices),), device_id_type=MESH
        ),
    )

    picks = slot_picks(owner_ref, count_ref[0], True)
    cell = cell_ref[...]
    digits = [cell // CELLS, cell // SIDE % SIDE, cell % SIDE]
    fields = [jnp.where(level_ref[...] == 0, mass_ref[...], -mass_ref[...])]
    for axis in range(3):
        fields.append(digits[axis].astype(F32) + frac_ref[axis])
    packed = jnp.dot(
        picks, jnp.concatenate(fields, axis=1), preferred_element_type=F32, precision=HIGHEST
    )
    for order in range(2):
        for field in range(4):
            part = packed[order * devices : (order + 1) * devices, field * 128 : field * 128 + 128]
            outbox[pl.ds(order * 4 + field, devices, stride=8), :] = part

    force = force_ref[...]
    planes = jnp.dot(force, plane_pick(BF16, False), preferred_element_type=F32)
    fronts = []
    for place in range(levels * 3):
        at = place * SIDE
        front = force_ref[at : at + 16, :].astype(F32)[0:1, :]
        fronts.append(jnp.concatenate([front, planes[at : at + 1, :]], axis=1))
    lower = planes + fold(jnp.concatenate(fronts, axis=0), BF16, None)
    force_gathered[lax.rem(me, INNER)] = lower.astype(BF16)

    pl.semaphore_wait(barrier, devices - 1)
    each(
        INNER, lambda step: inner_copy(force_gathered, inner_send, inner_recv, me, step).start()
    )

    def tile_copy(step):
        return block_copy(outbox, inbox, tile_send, tile_recv.at[step - 1], devices, me, step)

    each(devices, lambda step: tile_copy(step).start())
    own = pltpu.make_async_copy(outbox.at[block_rows(me)], inbox.at[block_rows(me)], own_sem)
    own.start()

    for level in range(levels):
        forward, backward = rim_sources(box_owner, level, devices)
        near[level] = forward
        near[levels + level] = backward
    table[0:rows, 0:CELLS] = force
    cross_a[...] = jnp.zeros_like(cross_a)
    cross_b[...] = jnp.zeros_like(cross_b)
    total[...] = jnp.zeros_like(total)
    kicks[...] = jnp.zeros_like(kicks)

    def force_relay():
        each(
            INNER, lambda step: inner_copy(force_gathered, inner_send, inner_recv, me, step).wait()
        )
        relay(
            near, 0, force_gathered, force_leaving, force_arrived, outer, levels, depth, me, BF16
        )
        each(
            outer,
            lambda step: outer_copy(
                force_leaving, force_arrived, outer_send, outer_recv, devices, me, step
            ).start(),
        )

    def mass_relay():
        each(
            INNER,
            lambda step: inner_copy(mass_gathered, inner_send2, inner_recv2, me, step).wait(),
        )
        relay(
            near, levels, mass_gathered, mass_leaving, mass_arrived, outer, levels, SIDE, me, F32
        )
        each(
            outer,
            lambda step: outer_copy(
                mass_leaving, mass_arrived, outer_send2, outer_recv2, devices, me, step
            ).start(),
        )

    def await_group(block, last):
        for part in range(SOURCES):
            if last and part == SOURCES - 1:
                own.wait()
            else:
                tile_copy(block * SOURCES + 1 + part).wait_recv()

    def fill(block, short, weighted):
        sources = group_sources(devices, me, block)
        fill_deposit(group_fields(inbox, sources), short, weighted)

    await_group(0, False)
    fill(0, short_a, weighted_a)

    def deposit_pair(pair, carry):
        @pl.when(pair == RELAY_AT)
        def _():
            force_relay()

        await_group(2 * pair + 1, False)
        await_group(2 * pair + 2, False)
        fill(2 * pair + 1, short_b, weighted_b)
        add_deposit(short_a, weighted_a, total)
        fill(2 * pair + 2, short_a, weighted_a)
        add_deposit(short_b, weighted_b, total)
        return carry

    lax.fori_loop(0, pairs - 1, deposit_pair, 0)
    await_group(groups - 1, True)
    fill(groups - 1, short_b, weighted_b)
    add_deposit(short_a, weighted_a, total)
    add_deposit(short_b, weighted_b, total)

    spread_deposit(total, wide)
    flipped = jnp.transpose(wide[...])
    density[...] = flipped[0 : levels * SIDE, 0:CELLS]
    beyond = flipped[levels * SIDE : levels * SIDE + levels, :]
    edge = iota((levels * SIDE, 128), 1) < 65
    upper = jnp.where(edge, flipped[0 : levels * SIDE, CELLS:WIDE], 0.0)
    mass_gathered[lax.rem(me, INNER)] = upper + fold(beyond, F32, HIGHEST)
    each(
        INNER, lambda step: inner_copy(mass_gathered, inner_send2, inner_recv2, me, step).start()
    )

    each(
        outer,
        lambda step: outer_copy(
            force_leaving, force_arrived, outer_send, outer_recv, devices, me, step
        ).wait(),
    )
    for level in range(levels):
        table[level * depth : (level + 1) * depth, CELLS:WIDE] = final_table(
            near, 0, force_arrived, level, depth, me, BF16
        )
    beyond = unfold(table[0:rows, CELLS:WIDE], BF16, None)
    beyond.append(jnp.zeros((16 - len(beyond), WIDE), F32))
    table[rows : rows + 16, :] = jnp.concatenate(beyond, axis=0).astype(BF16)

    def kick_copy(step):
        return back_copy(kicks, returned, kick_send, kick_recv, devices, me, step)

    def cross_of(block, cross):
        fill_cross(group_fields(inbox, group_sources(devices, me, block)), cross)

    def sample_of(block, cross):
        sources = group_sources(devices, me, block)
        sample(group_fields(inbox, sources), sources, table, cross, kicks)

    def send_group(block, last):
        for part in range(SOURCES - 1 if last else SOURCES):
            kick_copy(block * SOURCES + 1 + part).start()

    cross_of(0, cross_a)

    def sample_pair(pair, carry):
        @pl.when(pair == RELAY_AT)
        def _():
            mass_relay()

        cross_of(2 * pair + 1, cross_b)
        sample_of(2 * pair, cross_a)
        cross_of(2 * pair + 2, cross_a)
        sample_of(2 * pair + 1, cross_b)
        send_group(2 * pair, False)
        send_group(2 * pair + 1, False)
        return carry

    lax.fori_loop(0, pairs - 1, sample_pair, 0)
    cross_of(groups - 1, cross_b)
    sample_of(groups - 2, cross_a)
    sample_of(groups - 1, cross_b)
    send_group(groups - 2, False)
    send_group(groups - 1, True)
    kept = pltpu.make_async_copy(kicks.at[block_rows(me)], returned.at[block_rows(me)], own_sem)
    kept.start()

    picks = slot_picks(owner_ref, count_ref[0], False)
    each(
        outer,
        lambda step: outer_copy(
            mass_leaving, mass_arrived, outer_send2, outer_recv2, devices, me, step
        ).wait(),
    )
    rims = jnp.concatenate(
        [final_table(near, levels, mass_arrived, level, SIDE, me, F32) for level in range(levels)],
        axis=0,
    )
    beyond = unfold(rims, F32, HIGHEST)
    first_row = iota((SIDE, 1), 0) == 0
    low = [
        rims[level * SIDE : (level + 1) * SIDE, :]
        + jnp.where(first_row, beyond[level][:, CELLS:WIDE], 0.0)
        for level in range(levels)
    ]
    added = jnp.dot(
        jnp.concatenate(low, axis=0),
        plane_pick(F32, True),
        preferred_element_type=F32,
        precision=HIGHEST,
    )
    for level in range(levels):
        at = slice(level * SIDE, (level + 1) * SIDE)
        density[at, :] += added[at, :] + jnp.where(first_row, beyond[level][:, 0:CELLS], 0.0)

    all_blocks(outbox, inbox, tile_send, tile_recv.at[0], devices, me).wait_send()
    kept.wait()
    all_blocks(kicks, returned, kick_send, kick_recv, devices, me).wait()
    parts = []
    for order in range(2):
        columns = [returned[pl.ds(order * 4 + axis, devices, stride=8), :] for axis in range(3)]
        parts.append(jnp.concatenate(columns, axis=1))
    mine = jnp.dot(
        picks, jnp.concatenate(parts, axis=0), preferred_element_type=F32, precision=HIGHEST
    )
    for axis in range(3):
        kick[axis] = mine[:, axis * 128 : (axis + 1) * 128]


def on_device(
    tile_mass, tile_frac, tile_cell, tile_level, tile_owner, tile_count, box_owner, force_field
):
    devices = lax.axis_size("boxes")
    levels = box_owner.shape[0]
    tiles, width = tile_mass.shape
    rows = levels * 3 * SIDE
    outer = devices // INNER
    shape = jax.ShapeDtypeStruct
    vmem = pl.BlockSpec(memory_space=pltpu.VMEM)
    smem = pl.BlockSpec(memory_space=pltpu.SMEM)
    dma = pltpu.SemaphoreType.DMA
    blocks = pltpu.VMEM((devices * 8, width), F32)
    spread_rows = CHUNKS * 2 * SIDE + 16
    density, kick = pl.pallas_call(
        functools.partial(kernel, devices, levels),
        out_shape=(shape((levels * SIDE, CELLS), F32), shape((3, tiles, width), F32)),
        in_specs=[smem] + [vmem] * 7,
        out_specs=(vmem, vmem),
        scratch_shapes=[
            blocks,
            blocks,
            blocks,
            blocks,
            pltpu.VMEM((2 * levels, devices, 128), F32),
            pltpu.VMEM((INNER, rows, 128), BF16),
            pltpu.VMEM((outer, rows, 128), BF16),
            pltpu.VMEM((outer, rows, 128), BF16),
            pltpu.VMEM((INNER, levels * SIDE, 128), F32),
            pltpu.VMEM((outer, levels * SIDE, 128), F32),
            pltpu.VMEM((outer, levels * SIDE, 128), F32),
            pltpu.VMEM((rows + 16, WIDE), BF16),
            pltpu.VMEM((WIDE, LANES), BF16),
            pltpu.VMEM((WIDE, LANES), BF16),
            pltpu.VMEM((SHORT + 16, LANES), BF16),
            pltpu.VMEM((SHORT + 16, LANES), BF16),
            pltpu.VMEM((spread_rows, LANES), BF16),
            pltpu.VMEM((spread_rows, LANES), BF16),
            pltpu.VMEM((SHORT + 16, 256), F32),
            pltpu.VMEM((WIDE, 128), F32),
            dma,
            dma,
            dma((devices - 1,)),
            dma,
            dma,
            dma((INNER - 1,)),
            dma((INNER - 1,)),
            dma((outer - 1,)),
            dma((outer - 1,)),
            dma((INNER - 1,)),
            dma((INNER - 1,)),
            dma((outer - 1,)),
            dma((outer - 1,)),
        ],
        compiler_params=pltpu.CompilerParams(
            collective_id=0, has_side_effects=True, vmem_limit_bytes=48 << 20
        ),
        name="deposit_and_sample",
    )(
        tile_count,
        tile_owner.reshape(1, tiles),
        box_owner,
        tile_mass,
        jnp.transpose(tile_frac, (1, 0, 2)),
        tile_cell,
        tile_level,
        force_field.reshape(rows, CELLS),
    )
    return (density.reshape(levels, SIDE, CELLS), jnp.transpose(kick, (1, 0, 2)))


def solution(mesh):
    in_specs = (
        P("boxes", None),
        P("boxes", None, None),
        P("boxes", None),
        P("boxes", None),
        P("boxes", None),
        P("boxes"),
        P(),
        P(None, None, "boxes", None),
    )
    out_specs = (P(None, "boxes", None), P("boxes", None, None))
    return jax.shard_map(
        on_device, mesh=mesh, in_specs=in_specs, out_specs=out_specs, check_vma=False
    )
```

```python
import functools

import jax
import jax.numpy as jnp
import numpy as np
from jax import lax
from jax.experimental import pallas as pl
from jax.experimental.pallas import tpu as pltpu
from jax.sharding import PartitionSpec as P

MESH = pl.DeviceIdType.MESH
HIGHEST = lax.Precision.HIGHEST
F32 = jnp.float32
BF16 = jnp.bfloat16
LAT_X = 4
LAT_Z = 4
SIDE = 32
CELLS = SIDE * SIDE
WIDE = CELLS + 128
INNER = 8
SOURCES = 4
GROUP = 2 * SOURCES
LANES = GROUP * 128
CHUNK = 11
CHUNKS = 3
SHORT = (CHUNK + 1) * SIDE
FORCE_STAGES = (4, 8, 12)
MASS_STAGES = (3, 7, 10)

direction_table = np.array(
    [[1, 0, 0], [0, 1, 0], [0, 0, 1], [1, 1, 0], [1, 0, 1], [0, 1, 1], [1, 1, 1]], dtype=np.int32
)


def iota(shape, dim):
    return lax.broadcasted_iota(jnp.int32, shape, dim)


def ones_at(mask, dtype):
    return jnp.where(mask, 1.0, 0.0).astype(dtype)


def kind_of(value, parts):
    slab = value // 8
    group = slab // 5
    part = slab % 5
    kind = jnp.where(part == 3, 5, part)
    corner = value % 8
    kind = jnp.where(part == 4, jnp.where(corner == 0, 3, jnp.where(corner == 1, 4, 6)), kind)
    return group // parts, kind


def pack_rims(edges, fronts):
    lane = iota((8, 128), 1)
    row = iota((8, 128), 0)
    slabs = []
    for place, front in enumerate(fronts):
        pieces = [front[:, 128 * part : 128 * part + 128] for part in range(8)]
        slabs.append(jnp.concatenate(pieces, axis=0))
        for start in (0, 32, 64):
            total = None
            for part in range(4):
                at = place * SIDE + part * 8
                moved = pltpu.roll(edges[at : at + 8, :], (32 * part - start) % 128, 1)
                total = moved if total is None else jnp.where(lane >= 32 * part, moved, total)
            slabs.append(total)
        last = jnp.broadcast_to(front[:, CELLS:WIDE], (8, 128))
        corners = jnp.where(row == 0, last, pltpu.roll(last, 96, 1))
        slabs.append(jnp.where(row == 2, pltpu.roll(last, 64, 1), corners))
    return jnp.concatenate(slabs, axis=0)


def unpack_rims(values, amount):
    lane = iota((8, 128), 1)
    edges, fronts = [], []
    for place in range(amount):
        at = place * 40
        pieces = [values[at + part : at + part + 1, :] for part in range(8)]
        plane_y, plane_z, line = [values[at + 8 * n : at + 8 * n + 8, :] for n in (1, 2, 3)]
        for part in range(4):
            moved = pltpu.roll(plane_z, (32 - 32 * part) % 128, 1)
            moved = jnp.where(lane < 32, pltpu.roll(plane_y, (-32 * part) % 128, 1), moved)
            moved = jnp.where(lane == 64, pltpu.roll(line, (64 - 32 * part) % 128, 1), moved)
            edges.append(jnp.where(lane <= 64, moved, 0.0))
        corners = values[at + 32 : at + 40, :]
        first = jnp.where(lane < 32, corners, 0.0)[0:1, :]
        second = jnp.where((lane >= 32) & (lane < 64), pltpu.roll(corners, 32, 1), 0.0)[1:2, :]
        third = jnp.where(lane == 64, pltpu.roll(corners, 64, 1), 0.0)[2:3, :]
        fronts.append(jnp.concatenate(pieces + [first + second + third], axis=1))
    return jnp.concatenate(edges, axis=0), fronts


def plane_pick(dtype, flip):
    shape = (128, CELLS) if flip else (CELLS, 128)
    lane = iota(shape, 0 if flip else 1)
    cell = iota(shape, 1 if flip else 0)
    wanted = jnp.where(lane < 32, lane, jnp.where(lane < 64, (lane - 32) * SIDE, -1))
    wanted = jnp.where(lane == 64, 0, wanted)
    return ones_at(cell == wanted, dtype)


def slot_picks(owner_ref, count, by_slot):
    tiles = owner_ref.shape[1]
    across = jnp.broadcast_to(owner_ref[...], (tiles, tiles))
    down = jnp.transpose(across)
    same = across == down
    first, second = iota((tiles, tiles), 0), iota((tiles, tiles), 1)
    if by_slot:
        earlier = jnp.where(same & (first < second), 1.0, 0.0)
        rank = jnp.sum(earlier, axis=0, keepdims=True)
        fits = (across == first) & (second < count)
    else:
        earlier = jnp.where(same & (second < first), 1.0, 0.0)
        rank = jnp.sum(earlier, axis=1, keepdims=True)
        fits = (down == second) & (first < count)
    picks = [jnp.where(fits & (rank == float(order)), 1.0, 0.0) for order in range(2)]
    return jnp.concatenate(picks, axis=0 if by_slot else 1)


def rim_sources(box_owner, level, devices):
    lat_y = devices // (LAT_X * LAT_Z)
    square = (devices, devices)
    across = jnp.broadcast_to(box_owner[level : level + 1, :], square)
    down = jnp.transpose(across).astype(F32).astype(BF16)
    hot = ones_at(across == iota(square, 0), BF16)
    places = iota(square, 0).astype(F32).astype(BF16)
    box = jnp.dot(hot, places, preferred_element_type=F32).astype(jnp.int32)
    at = [box // (lat_y * LAT_Z), box // LAT_Z % lat_y, box % LAT_Z]
    found = []
    for sign in (1, -1):
        hots = []
        for step in direction_table:
            near = [
                (at[axis] + (sign * int(step[axis]) + extent)) % extent
                for axis, extent in enumerate((LAT_X, lat_y, LAT_Z))
            ]
            wanted = (near[0] * lat_y + near[1]) * LAT_Z + near[2]
            hots.append(ones_at(wanted == iota(square, 1), BF16))
        owners = jnp.dot(jnp.concatenate(hots, axis=0), down, preferred_element_type=F32)
        found.append(ones_at(owners == iota(owners.shape, 1).astype(F32), BF16))
    return found


def choose(hots, values, parts, devices):
    levels = hots.shape[0] // (7 * devices)
    width = values.shape[1]
    level_of, kind = kind_of(iota((1, width), 1), parts)
    total = jnp.zeros((devices, width), F32)
    for level in range(levels):
        at = level * 7 * devices
        found = jnp.dot(hots[at : at + 7 * devices, :], values, preferred_element_type=F32)
        for direction in range(7):
            part = found[direction * devices : (direction + 1) * devices, :]
            total = jnp.where((level_of == level) & (kind == direction), part, total)
    return total


def each(count, act):
    def body(step, carry):
        act(step)
        return carry

    lax.fori_loop(1, count, body, 0)


def block_rows(device):
    return pl.ds(pl.multiple_of(device * 8, 8), 8)


def block_copy(source, target, send, recv, devices, me, step):
    peer = lax.rem(me + step, devices)
    return pltpu.make_async_remote_copy(
        src_ref=source.at[block_rows(peer)],
        dst_ref=target.at[block_rows(me)],
        send_sem=send,
        recv_sem=recv,
        device_id=(peer,),
        device_id_type=MESH,
    )


def back_copy(source, target, send, recv, devices, me, step):
    peer = lax.rem(me + devices - step, devices)
    return pltpu.make_async_remote_copy(
        src_ref=source.at[block_rows(peer)],
        dst_ref=target.at[block_rows(me)],
        send_sem=send,
        recv_sem=recv,
        device_id=(peer,),
        device_id_type=MESH,
    )


def all_blocks(source, target, send, recv, devices, me):
    rows = (devices - 1) * 8
    return pltpu.make_async_remote_copy(
        src_ref=source.at[pl.ds(0, rows)],
        dst_ref=target.at[pl.ds(0, rows)],
        send_sem=send,
        recv_sem=recv,
        device_id=(lax.rem(me + 1, devices),),
        device_id_type=MESH,
    )


def rim_hops(source, middle, target, sems, devices, me):
    rows = devices // INNER
    row, place = me // INNER, lax.rem(me, INNER)

    def first(step):
        other = lax.rem(place + step, INNER)
        return pltpu.make_async_remote_copy(
            src_ref=source.at[:, other],
            dst_ref=middle.at[place],
            send_sem=sems.at[0],
            recv_sem=sems.at[1],
            device_id=(row * INNER + other,),
            device_id_type=MESH,
        )

    def second(step):
        other = lax.rem(row + step, rows)
        return pltpu.make_async_remote_copy(
            src_ref=middle.at[:, other],
            dst_ref=target.at[row],
            send_sem=sems.at[2],
            recv_sem=sems.at[3],
            device_id=(other * INNER + place,),
            device_id_type=MESH,
        )

    def start():
        each(INNER, lambda step: first(step).start())
        middle[place] = source[:, place]

    def forward():
        pltpu.make_async_remote_copy(
            src_ref=middle.at[pl.ds(0, INNER - 1)],
            dst_ref=middle.at[pl.ds(0, INNER - 1)],
            send_sem=sems.at[0],
            recv_sem=sems.at[1],
            device_id=(row * INNER + lax.rem(place + 1, INNER),),
            device_id_type=MESH,
        ).wait()
        each(rows, lambda step: second(step).start())
        target[row] = middle[:, row]

    def finish():
        pltpu.make_async_remote_copy(
            src_ref=target.at[pl.ds(0, rows - 1)],
            dst_ref=target.at[pl.ds(0, rows - 1)],
            send_sem=sems.at[2],
            recv_sem=sems.at[3],
            device_id=(lax.rem(row + 1, rows) * INNER + place,),
            device_id_type=MESH,
        ).wait()

    return start, forward, finish


def hat(coord, rows, start):
    ids = iota((rows, coord.shape[1]), 0).astype(F32) + start
    return jnp.maximum(0.0, 1.0 - jnp.abs(coord - ids))


def group_sources(devices, me, block):
    return [lax.rem(me + devices - (block * SOURCES + 1 + part), devices) for part in range(SOURCES)]


def group_fields(inbox, sources):
    fields = []
    for field in range(4):
        rows = []
        for source in sources:
            for order in range(2):
                rows.append(inbox[pl.ds(source * 8 + (order * 4 + field), 1), :])
        fields.append(jnp.concatenate(rows, axis=1))
    return fields


def fill_deposit(fields, short, weighted):
    mass, x, y, z = fields
    chunk = jnp.where(y >= 2.0 * CHUNK, 2.0, jnp.where(y >= CHUNK, 1.0, 0.0))
    hat_y = hat(y - chunk * CHUNK, 16, 0.0)
    hat_z = hat(z, SIDE, 0.0)
    for row in range(CHUNK + 1):
        short[row * SIDE : (row + 1) * SIDE, :] = (hat_y[row : row + 1, :] * hat_z).astype(BF16)
    tops = jnp.where(iota((16, LANES), 0) <= CHUNK, hat_y * hat(z, 1, float(SIDE)), 0.0)
    short[SHORT : SHORT + 16, :] = tops.astype(BF16)
    hat_x = hat(x, SIDE, 0.0)
    for place in range(CHUNKS):
        for level in range(2):
            own = jnp.maximum(mass if level == 0 else -mass, 0.0)
            own = jnp.where(chunk == float(place), own, 0.0)
            at = (place * 2 + level) * SIDE
            weighted[at : at + SIDE, :] = (own * hat_x).astype(BF16)
    row_of = 2.0 * chunk + jnp.where(mass < 0.0, 1.0, 0.0)
    ends = jnp.where(iota((16, LANES), 0).astype(F32) == row_of, jnp.abs(mass), 0.0)
    at = CHUNKS * 2 * SIDE
    weighted[at : at + 16, :] = (ends * hat(x, 1, float(SIDE))).astype(BF16)


def add_deposit(short, weighted, total):
    product = lax.dot_general(
        short[...], weighted[...], (((1,), (1,)), ((), ())), preferred_element_type=F32
    )
    total[:, 0 : product.shape[1]] += product


def fill_cross(fields, cross):
    _, _, y, z = fields
    hat_y, hat_z = hat(y, SIDE, 0.0), hat(z, SIDE, 0.0)
    end_y, end_z = hat(y, 1, float(SIDE)), hat(z, 1, float(SIDE))
    for row in range(SIDE):
        cross[row * SIDE : (row + 1) * SIDE, :] = (hat_y[row : row + 1, :] * hat_z).astype(BF16)
    cross[CELLS : CELLS + 32, :] = (end_y * hat_z).astype(BF16)
    cross[CELLS + 32 : CELLS + 64, :] = (hat_y * end_z).astype(BF16)
    last = jnp.where(iota((16, LANES), 0) == 0, end_y * end_z, 0.0)
    cross[CELLS + 64 : CELLS + 80, :] = last.astype(BF16)


def sample(fields, sources, table, cross, kicks):
    mass, x, _, _ = fields
    rows = table.shape[0] - 16
    depth = rows // 2
    sampled = jnp.dot(table[...], cross[...], preferred_element_type=F32)
    hat_x, end_x = hat(x, SIDE, 0.0), hat(x, 1, float(SIDE))
    upper_level = mass < 0.0
    for axis in range(3):
        at = axis * SIDE
        picked = jnp.where(
            upper_level, sampled[depth + at : depth + at + SIDE, :], sampled[at : at + SIDE, :]
        )
        at = rows + axis
        far = jnp.where(upper_level, sampled[at + 3 : at + 4, :], sampled[at : at + 1, :])
        value = jnp.sum(hat_x * picked, axis=0, keepdims=True) + end_x * far
        for part, source in enumerate(sources):
            for order in range(2):
                lanes = slice((part * 2 + order) * 128, (part * 2 + order + 1) * 128)
                kicks[pl.ds(source * 8 + (order * 4 + axis), 1), :] = value[:, lanes]


def spread_deposit(total, wide):
    wide[...] = jnp.zeros_like(wide)
    first, second = total[:, 0:128], total[:, 128:256]
    low = iota(first.shape, 1) < 2 * SIDE
    for place in range(CHUNKS):
        main = [first, pltpu.roll(first, 64, 1), second][place]
        ends = second if place == 0 else pltpu.roll(second, 128 - 2 * place, 1)
        both = jnp.where(low, main, ends)
        at = place * CHUNK * SIDE
        wide[at : at + SHORT, :] += both[0:SHORT, :]
        at = CELLS + SIDE + place * CHUNK
        wide[at : at + CHUNK + 1, :] += both[SHORT : SHORT + CHUNK + 1, :]


def kernel(
    devices,
    levels,
    count_ref,
    owner_ref,
    box_owner,
    mass_in,
    frac_in,
    cell_in,
    level_in,
    force_in,
    density,
    kick,
    outbox,
    inbox,
    kicks,
    returned,
    mass_ref,
    frac_ref,
    cell_ref,
    level_ref,
    force_ref,
    hots,
    force_out,
    force_spread,
    force_next,
    force_last,
    mass_out,
    mass_spread,
    mass_next,
    mass_last,
    force_middle,
    mass_middle,
    table,
    cross_a,
    cross_b,
    short_a,
    short_b,
    weighted_a,
    weighted_b,
    total,
    wide,
    own_sem,
    tile_send,
    tile_recv,
    kick_send,
    kick_recv,
    load_sem,
    rim_sems,
):
    me = lax.axis_index("boxes")
    depth = 3 * SIDE
    rows = levels * depth
    groups = devices // SOURCES
    pairs = groups // 2

    loads = [
        pltpu.make_async_copy(source, target, load_sem.at[place])
        for place, (source, target) in enumerate(
            [
                (mass_in, mass_ref),
                (frac_in, frac_ref),
                (cell_in, cell_ref),
                (level_in, level_ref),
                (force_in, force_ref),
            ]
        )
    ]
    for load in loads:
        load.start()
    barrier = pltpu.get_barrier_semaphore()
    each(
        devices,
        lambda step: pl.semaphore_signal(
            barrier, inc=1, device_id=(lax.rem(me + step, devices),), device_id_type=MESH
        ),
    )

    picks = slot_picks(owner_ref, count_ref[0], True)
    for load in loads[:4]:
        load.wait()
    cell = cell_ref[...]
    digits = [cell // CELLS, cell // SIDE % SIDE, cell % SIDE]
    fields = [jnp.where(level_ref[...] == 0, mass_ref[...], -mass_ref[...])]
    for axis in range(3):
        fields.append(digits[axis].astype(F32) + frac_ref[axis])
    packed = jnp.dot(
        picks, jnp.concatenate(fields, axis=1), preferred_element_type=F32, precision=HIGHEST
    )
    for order in range(2):
        for field in range(4):
            part = packed[order * devices : (order + 1) * devices, field * 128 : field * 128 + 128]
            outbox[pl.ds(order * 4 + field, devices, stride=8), :] = part

    pl.semaphore_wait(barrier, devices - 1)

    force_hops = [
        rim_hops(force_out, force_middle.at[0], force_spread, rim_sems.at[0], devices, me),
        rim_hops(force_next, force_middle.at[1], force_last, rim_sems.at[1], devices, me),
    ]
    mass_hops = [
        rim_hops(mass_out, mass_middle.at[0], mass_spread, rim_sems.at[2], devices, me),
        rim_hops(mass_next, mass_middle.at[1], mass_last, rim_sems.at[3], devices, me),
    ]

    def tile_copy(step):
        group = (step - 1) // SOURCES
        return block_copy(outbox, inbox, tile_send, tile_recv.at[group], devices, me, step)

    each(devices, lambda step: tile_copy(step).start())
    own = pltpu.make_async_copy(outbox.at[block_rows(me)], inbox.at[block_rows(me)], own_sem)
    own.start()

    loads[4].wait()
    force = force_ref[...]
    edges = jnp.dot(force, plane_pick(BF16, False), preferred_element_type=F32)
    fronts = []
    for place in range(levels * 3):
        at = place * SIDE
        front = force_ref[at : at + 16, :].astype(F32)[0:1, :]
        fronts.append(jnp.concatenate([front, edges[at : at + 1, :]], axis=1))
    values = pack_rims(edges, fronts)
    values = jnp.concatenate([values, jnp.zeros((256 - values.shape[0], 128), F32)], axis=0)
    for half in range(2):
        block = jnp.transpose(values[half * 128 : half * 128 + 128, :])
        force_out[:, :, half, :] = block.reshape(devices // INNER, INNER, 128)
    force_hops[0][0]()

    for level in range(levels):
        ways = rim_sources(box_owner, level, devices)
        for way in range(2):
            hots[pl.ds((way * levels + level) * 7 * devices, 7 * devices), :] = ways[way]
    table[0:rows, 0:CELLS] = force
    blank = jnp.zeros((WIDE - CELLS - 80, LANES), BF16)
    cross_a[CELLS + 80 : WIDE, :] = blank
    cross_b[CELLS + 80 : WIDE, :] = blank
    total[...] = jnp.zeros_like(total)
    kicks[...] = jnp.zeros_like(kicks)

    def force_relay():
        force_hops[0][2]()
        values = jnp.concatenate(
            [force_spread[:, :, half, :].reshape(devices, 128) for half in range(2)], axis=1
        )
        chosen = choose(hots[0 : levels * 7 * devices, :], values.astype(BF16), 3, devices)
        for half in range(2):
            block = chosen[:, half * 128 : half * 128 + 128]
            force_next[:, :, half, :] = block.reshape(devices // INNER, INNER, 128)
        force_hops[1][0]()

    def mass_relay():
        mass_hops[0][2]()
        values = mass_spread[:, :, 0, :].reshape(devices, 128)
        high = values.astype(BF16)
        rest = (values - high.astype(F32)).astype(BF16)
        way = hots[levels * 7 * devices : 2 * levels * 7 * devices, :]
        chosen = choose(way, high, 1, devices) + choose(way, rest, 1, devices)
        mass_next[:, :, 0, :] = chosen.reshape(devices // INNER, INNER, 128)
        mass_hops[1][0]()

    def stages(pair, at, acts):
        for place, act in zip(at, acts):
            pl.when(pair == place)(act)

    def await_group(block, last):
        if last:
            own.wait()
        amount = (SOURCES - 1 if last else SOURCES) * 8
        pltpu.make_async_remote_copy(
            src_ref=outbox.at[pl.ds(0, amount)],
            dst_ref=inbox.at[pl.ds(0, amount)],
            send_sem=tile_send,
            recv_sem=tile_recv.at[block],
            device_id=(lax.rem(me + 1, devices),),
            device_id_type=MESH,
        ).wait_recv()

    def fill(block, short, weighted):
        sources = group_sources(devices, me, block)
        fill_deposit(group_fields(inbox, sources), short, weighted)

    await_group(0, False)
    fill(0, short_a, weighted_a)

    def deposit_pair(pair, carry):
        stages(pair, FORCE_STAGES, (force_hops[0][1], force_relay, force_hops[1][1]))
        await_group(2 * pair + 1, False)
        await_group(2 * pair + 2, False)
        fill(2 * pair + 1, short_b, weighted_b)
        add_deposit(short_a, weighted_a, total)
        fill(2 * pair + 2, short_a, weighted_a)
        add_deposit(short_b, weighted_b, total)
        return carry

    lax.fori_loop(0, pairs - 1, deposit_pair, 0)
    await_group(groups - 1, True)
    fill(groups - 1, short_b, weighted_b)
    add_deposit(short_a, weighted_a, total)
    add_deposit(short_b, weighted_b, total)

    spread_deposit(total, wide)
    flipped = jnp.transpose(wide[...])
    density[...] = flipped[0 : levels * SIDE, 0:CELLS]
    beyond = flipped[levels * SIDE : levels * SIDE + levels, :]
    values = pack_rims(
        flipped[0 : levels * SIDE, CELLS:WIDE],
        [beyond[level : level + 1, :] for level in range(levels)],
    )
    values = jnp.concatenate([values, jnp.zeros((128 - values.shape[0], 128), F32)], axis=0)
    mass_out[:, :, 0, :] = jnp.transpose(values).reshape(devices // INNER, INNER, 128)
    mass_hops[0][0]()

    force_hops[1][2]()
    values = jnp.concatenate(
        [jnp.transpose(force_last[:, :, half, :].reshape(devices, 128)) for half in range(2)],
        axis=0,
    )
    edges, fronts = unpack_rims(values, levels * 3)
    table[0:rows, CELLS:WIDE] = edges.astype(BF16)
    fronts.append(jnp.zeros((16 - len(fronts), WIDE), F32))
    table[rows : rows + 16, :] = jnp.concatenate(fronts, axis=0).astype(BF16)

    def kick_copy(step):
        return back_copy(kicks, returned, kick_send, kick_recv, devices, me, step)

    def cross_of(block, cross):
        fill_cross(group_fields(inbox, group_sources(devices, me, block)), cross)

    def sample_of(block, cross):
        sources = group_sources(devices, me, block)
        sample(group_fields(inbox, sources), sources, table, cross, kicks)

    def send_group(block, last):
        for part in range(SOURCES - 1 if last else SOURCES):
            kick_copy(block * SOURCES + 1 + part).start()

    cross_of(0, cross_a)

    def sample_pair(pair, carry):
        stages(pair, MASS_STAGES, (mass_hops[0][1], mass_relay, mass_hops[1][1]))
        cross_of(2 * pair + 1, cross_b)
        sample_of(2 * pair, cross_a)
        cross_of(2 * pair + 2, cross_a)
        sample_of(2 * pair + 1, cross_b)
        send_group(2 * pair, False)
        send_group(2 * pair + 1, False)
        return carry

    lax.fori_loop(0, pairs - 1, sample_pair, 0)
    cross_of(groups - 1, cross_b)
    sample_of(groups - 2, cross_a)
    sample_of(groups - 1, cross_b)
    send_group(groups - 2, False)
    send_group(groups - 1, True)
    kept = pltpu.make_async_copy(kicks.at[block_rows(me)], returned.at[block_rows(me)], own_sem)
    kept.start()

    picks = slot_picks(owner_ref, count_ref[0], False)
    mass_hops[1][2]()
    values = jnp.transpose(mass_last[:, :, 0, :].reshape(devices, 128))
    edges, fronts = unpack_rims(values, levels)
    first_row = iota((SIDE, 1), 0) == 0
    low = [
        edges[level * SIDE : (level + 1) * SIDE, :]
        + jnp.where(first_row, fronts[level][:, CELLS:WIDE], 0.0)
        for level in range(levels)
    ]
    added = jnp.dot(
        jnp.concatenate(low, axis=0),
        plane_pick(F32, True),
        preferred_element_type=F32,
        precision=HIGHEST,
    )
    for level in range(levels):
        at = slice(level * SIDE, (level + 1) * SIDE)
        density[at, :] += added[at, :] + jnp.where(first_row, fronts[level][:, 0:CELLS], 0.0)

    all_blocks(outbox, inbox, tile_send, tile_recv.at[0], devices, me).wait_send()
    kept.wait()
    all_blocks(kicks, returned, kick_send, kick_recv, devices, me).wait()
    parts = []
    for order in range(2):
        columns = [returned[pl.ds(order * 4 + axis, devices, stride=8), :] for axis in range(3)]
        parts.append(jnp.concatenate(columns, axis=1))
    mine = jnp.dot(
        picks, jnp.concatenate(parts, axis=0), preferred_element_type=F32, precision=HIGHEST
    )
    for axis in range(3):
        kick[axis] = mine[:, axis * 128 : (axis + 1) * 128]


def on_device(
    tile_mass, tile_frac, tile_cell, tile_level, tile_owner, tile_count, box_owner, force_field
):
    devices = lax.axis_size("boxes")
    levels = box_owner.shape[0]
    tiles, width = tile_mass.shape
    rows = levels * 3 * SIDE
    shape = jax.ShapeDtypeStruct
    vmem = pl.BlockSpec(memory_space=pltpu.VMEM)
    smem = pl.BlockSpec(memory_space=pltpu.SMEM)
    dma = pltpu.SemaphoreType.DMA
    blocks = pltpu.VMEM((devices * 8, width), F32)
    spread_rows = CHUNKS * 2 * SIDE + 16
    density, kick = pl.pallas_call(
        functools.partial(kernel, devices, levels),
        out_shape=(shape((levels * SIDE, CELLS), F32), shape((3, tiles, width), F32)),
        in_specs=[smem, vmem, vmem] + [pl.BlockSpec(memory_space=pl.ANY)] * 5,
        out_specs=(vmem, vmem),
        scratch_shapes=[
            blocks,
            blocks,
            blocks,
            blocks,
            pltpu.VMEM((tiles, width), F32),
            pltpu.VMEM((3, tiles, width), F32),
            pltpu.VMEM((tiles, width), jnp.int32),
            pltpu.VMEM((tiles, width), jnp.int32),
            pltpu.VMEM((rows, CELLS), BF16),
            pltpu.VMEM((2 * levels * 7 * devices, devices), BF16),
        ]
        + [pltpu.VMEM((devices // INNER, INNER, 2, 128), F32)] * 4
        + [pltpu.VMEM((devices // INNER, INNER, 1, 128), F32)] * 4
        + [
            pltpu.VMEM((2, INNER, devices // INNER, 2, 128), F32),
            pltpu.VMEM((2, INNER, devices // INNER, 1, 128), F32),
        ]
        + [
            pltpu.VMEM((rows + 16, WIDE), BF16),
            pltpu.VMEM((WIDE, LANES), BF16),
            pltpu.VMEM((WIDE, LANES), BF16),
            pltpu.VMEM((SHORT + 16, LANES), BF16),
            pltpu.VMEM((SHORT + 16, LANES), BF16),
            pltpu.VMEM((spread_rows, LANES), BF16),
            pltpu.VMEM((spread_rows, LANES), BF16),
            pltpu.VMEM((SHORT + 16, 256), F32),
            pltpu.VMEM((WIDE, 128), F32),
            dma,
            dma,
            dma((devices // SOURCES,)),
            dma,
            dma,
            dma((5,)),
            dma((4, 4)),
        ],
        compiler_params=pltpu.CompilerParams(
            collective_id=0, has_side_effects=True, vmem_limit_bytes=60 << 20
        ),
        name="deposit_and_sample",
    )(
        tile_count,
        tile_owner.reshape(1, tiles),
        box_owner,
        tile_mass,
        jnp.transpose(tile_frac, (1, 0, 2)),
        tile_cell,
        tile_level,
        force_field.reshape(rows, CELLS),
    )
    return (density.reshape(levels, SIDE, CELLS), jnp.transpose(kick, (1, 0, 2)))


def solution(mesh):
    in_specs = (
        P("boxes", None),
        P("boxes", None, None),
        P("boxes", None),
        P("boxes", None),
        P("boxes", None),
        P("boxes"),
        P(),
        P(None, None, "boxes", None),
    )
    out_specs = (P(None, "boxes", None), P("boxes", None, None))
    return jax.shard_map(
        on_device, mesh=mesh, in_specs=in_specs, out_specs=out_specs, check_vma=False
    )
```

```python
import functools

import jax
import jax.numpy as jnp
import numpy as np
from jax import lax
from jax.experimental import pallas as pl
from jax.experimental.pallas import tpu as pltpu
from jax.sharding import PartitionSpec as P

MESH = pl.DeviceIdType.MESH
F32 = jnp.float32
BF16 = jnp.bfloat16
LAT_X = 4
LAT_Z = 4
SIDE = 32
CELLS = SIDE * SIDE
WIDE = CELLS + 128
INNER = 8
GROUP = 2 * INNER
LANES = GROUP * 128
CHUNK = 11
CHUNKS = 3
SHORT = (CHUNK + 1) * SIDE
FORCE_STAGES = (4, 6)
MASS_STAGES = (1, 3, 5)

direction_table = np.array(
    [[1, 0, 0], [0, 1, 0], [0, 0, 1], [1, 1, 0], [1, 0, 1], [0, 1, 1], [1, 1, 1]], dtype=np.int32
)


def iota(shape, dim):
    return lax.broadcasted_iota(jnp.int32, shape, dim)


def ones_at(mask, dtype):
    return jnp.where(mask, 1.0, 0.0).astype(dtype)


def exact_dot(picks, values):
    width = values.shape[1]
    high = values.astype(BF16)
    rest = values - high.astype(F32)
    middle = rest.astype(BF16)
    low = (rest - middle.astype(F32)).astype(BF16)
    parts = jnp.concatenate([high, middle, low], axis=1)
    found = jnp.dot(picks, parts, preferred_element_type=F32)
    return (found[:, 0:width] + found[:, width : 2 * width]) + found[:, 2 * width : 3 * width]


def kind_of(value, parts):
    slab = value // 8
    group = slab // 5
    part = slab % 5
    kind = jnp.where(part == 3, 5, part)
    corner = value % 8
    kind = jnp.where(part == 4, jnp.where(corner == 0, 3, jnp.where(corner == 1, 4, 6)), kind)
    return group // parts, kind


def pack_rims(edges, fronts):
    lane = iota((8, 128), 1)
    row = iota((8, 128), 0)
    slabs = []
    for place, front in enumerate(fronts):
        pieces = [front[:, 128 * part : 128 * part + 128] for part in range(8)]
        slabs.append(jnp.concatenate(pieces, axis=0))
        for start in (0, 32, 64):
            total = None
            for part in range(4):
                at = place * SIDE + part * 8
                moved = pltpu.roll(edges[at : at + 8, :], (32 * part - start) % 128, 1)
                total = moved if total is None else jnp.where(lane >= 32 * part, moved, total)
            slabs.append(total)
        last = jnp.broadcast_to(front[:, CELLS:WIDE], (8, 128))
        corners = jnp.where(row == 0, last, pltpu.roll(last, 96, 1))
        slabs.append(jnp.where(row == 2, pltpu.roll(last, 64, 1), corners))
    return jnp.concatenate(slabs, axis=0)


def unpack_rims(values, amount):
    lane = iota((8, 128), 1)
    edges, fronts = [], []
    for place in range(amount):
        at = place * 40
        pieces = [values[at + part : at + part + 1, :] for part in range(8)]
        plane_y, plane_z, line = [values[at + 8 * n : at + 8 * n + 8, :] for n in (1, 2, 3)]
        for part in range(4):
            moved = pltpu.roll(plane_z, (32 - 32 * part) % 128, 1)
            moved = jnp.where(lane < 32, pltpu.roll(plane_y, (-32 * part) % 128, 1), moved)
            moved = jnp.where(lane == 64, pltpu.roll(line, (64 - 32 * part) % 128, 1), moved)
            edges.append(jnp.where(lane <= 64, moved, 0.0))
        corners = values[at + 32 : at + 40, :]
        first = jnp.where(lane < 32, corners, 0.0)[0:1, :]
        second = jnp.where((lane >= 32) & (lane < 64), pltpu.roll(corners, 32, 1), 0.0)[1:2, :]
        third = jnp.where(lane == 64, pltpu.roll(corners, 64, 1), 0.0)[2:3, :]
        fronts.append(jnp.concatenate(pieces + [first + second + third], axis=1))
    return jnp.concatenate(edges, axis=0), fronts


def plane_pick(dtype, flip):
    shape = (128, CELLS) if flip else (CELLS, 128)
    lane = iota(shape, 0 if flip else 1)
    cell = iota(shape, 1 if flip else 0)
    wanted = jnp.where(lane < 32, lane, jnp.where(lane < 64, (lane - 32) * SIDE, -1))
    wanted = jnp.where(lane == 64, 0, wanted)
    return ones_at(cell == wanted, dtype)


def slot_picks(owner_ref, count, by_slot):
    tiles = owner_ref.shape[1]
    across = jnp.broadcast_to(owner_ref[...], (tiles, tiles))
    down = jnp.transpose(across)
    same = across == down
    first, second = iota((tiles, tiles), 0), iota((tiles, tiles), 1)
    if by_slot:
        earlier = jnp.where(same & (first < second), 1.0, 0.0)
        rank = jnp.sum(earlier, axis=0, keepdims=True)
        fits = (across == first) & (second < count)
    else:
        earlier = jnp.where(same & (second < first), 1.0, 0.0)
        rank = jnp.sum(earlier, axis=1, keepdims=True)
        fits = (down == second) & (first < count)
    picks = [jnp.where(fits & (rank == float(order)), 1.0, 0.0) for order in range(2)]
    return jnp.concatenate(picks, axis=0 if by_slot else 1).astype(BF16)


def rim_sources(box_owner, level, devices):
    lat_y = devices // (LAT_X * LAT_Z)
    square = (devices, devices)
    across = jnp.broadcast_to(box_owner[level : level + 1, :], square)
    down = jnp.transpose(across).astype(F32).astype(BF16)
    hot = ones_at(across == iota(square, 0), BF16)
    places = iota(square, 0).astype(F32).astype(BF16)
    box = jnp.dot(hot, places, preferred_element_type=F32).astype(jnp.int32)
    at = [box // (lat_y * LAT_Z), box // LAT_Z % lat_y, box % LAT_Z]
    found = []
    for sign in (1, -1):
        hots = []
        for step in direction_table:
            near = [
                (at[axis] + (sign * int(step[axis]) + extent)) % extent
                for axis, extent in enumerate((LAT_X, lat_y, LAT_Z))
            ]
            wanted = (near[0] * lat_y + near[1]) * LAT_Z + near[2]
            hots.append(ones_at(wanted == iota(square, 1), BF16))
        owners = jnp.dot(jnp.concatenate(hots, axis=0), down, preferred_element_type=F32)
        found.append(ones_at(owners == iota(owners.shape, 1).astype(F32), BF16))
    return found


def choose(hots, values, parts, devices):
    levels = hots.shape[0] // (7 * devices)
    width = values.shape[1]
    level_of, kind = kind_of(iota((1, width), 1) % (128 if parts == 1 else 256), parts)
    total = jnp.zeros((devices, width), F32)
    for level in range(levels):
        at = level * 7 * devices
        found = jnp.dot(hots[at : at + 7 * devices, :], values, preferred_element_type=F32)
        for direction in range(7):
            part = found[direction * devices : (direction + 1) * devices, :]
            total = jnp.where((level_of == level) & (kind == direction), part, total)
    return total


def each(count, act):
    def body(step, carry):
        act(step)
        return carry

    lax.fori_loop(1, count, body, 0)


def block_rows(device):
    return pl.ds(pl.multiple_of(device * 8, 8), 8)


def block_copy(source, target, send, recv, peer, me):
    return pltpu.make_async_remote_copy(
        src_ref=source.at[block_rows(peer)],
        dst_ref=target.at[block_rows(me)],
        send_sem=send,
        recv_sem=recv,
        device_id=(peer,),
        device_id_type=MESH,
    )


def all_blocks(source, target, send, recv, devices, me):
    rows = (devices - 1) * 8
    return pltpu.make_async_remote_copy(
        src_ref=source.at[pl.ds(0, rows)],
        dst_ref=target.at[pl.ds(0, rows)],
        send_sem=send,
        recv_sem=recv,
        device_id=(lax.rem(me + 1, devices),),
        device_id_type=MESH,
    )


def rim_hops(source, middle, target, sems, devices, me):
    rows = devices // INNER
    row, place = me // INNER, lax.rem(me, INNER)

    def first(step):
        other = lax.rem(place + step, INNER)
        return pltpu.make_async_remote_copy(
            src_ref=source.at[:, other],
            dst_ref=middle.at[place],
            send_sem=sems.at[0],
            recv_sem=sems.at[1],
            device_id=(row * INNER + other,),
            device_id_type=MESH,
        )

    def second(step):
        other = lax.rem(row + step, rows)
        return pltpu.make_async_remote_copy(
            src_ref=middle.at[:, other],
            dst_ref=target.at[row],
            send_sem=sems.at[2],
            recv_sem=sems.at[3],
            device_id=(other * INNER + place,),
            device_id_type=MESH,
        )

    def start():
        each(INNER, lambda step: first(step).start())
        middle[place] = source[:, place]

    def forward():
        pltpu.make_async_remote_copy(
            src_ref=middle.at[pl.ds(0, INNER - 1)],
            dst_ref=middle.at[pl.ds(0, INNER - 1)],
            send_sem=sems.at[0],
            recv_sem=sems.at[1],
            device_id=(row * INNER + lax.rem(place + 1, INNER),),
            device_id_type=MESH,
        ).wait()
        each(rows, lambda step: second(step).start())
        target[row] = middle[:, row]

    def finish():
        pltpu.make_async_remote_copy(
            src_ref=target.at[pl.ds(0, rows - 1)],
            dst_ref=target.at[pl.ds(0, rows - 1)],
            send_sem=sems.at[2],
            recv_sem=sems.at[3],
            device_id=(lax.rem(row + 1, rows) * INNER + place,),
            device_id_type=MESH,
        ).wait()

    return start, forward, finish


def hat(coord, rows):
    ids = iota((rows, coord.shape[1]), 0).astype(F32)
    return jnp.maximum(0.0, 1.0 - jnp.abs(coord - ids))


def group_fields(inbox, first):
    return [inbox[pl.ds(first + field, GROUP, stride=4), :] for field in range(4)]


def flat(ref, first, stride):
    return jnp.concatenate([ref[pl.ds(first + t * stride, 1), :] for t in range(GROUP)], axis=1)


def end_hat(coord):
    return jnp.maximum(0.0, 1.0 - jnp.abs(coord - float(SIDE)))


def keep(rows, values):
    for place, value in enumerate(values):
        rows[place * GROUP : (place + 1) * GROUP, :] = value
    return [flat(rows, place * GROUP, 1) for place in range(len(values))]


def fill_deposit(inbox, first, rows, short, weighted):
    mass, x, y, z = group_fields(inbox, first)
    chunk = jnp.where(y >= 2.0 * CHUNK, 2.0, jnp.where(y >= CHUNK, 1.0, 0.0))
    row_of = 2.0 * chunk + jnp.where(mass < 0.0, 1.0, 0.0)
    size = jnp.abs(mass)
    owns = [jnp.where(row_of == float(place), size, 0.0) for place in range(CHUNKS * 2)]
    rest = [y - chunk * CHUNK, end_hat(z), row_of, size * end_hat(x)]
    *owns, near_y, end_z, row_of, end_x = keep(rows, owns + rest)
    hat_x = hat(flat(inbox, first + 1, 4), SIDE)
    hat_y = hat(near_y, 16)
    hat_z = hat(flat(inbox, first + 3, 4), SIDE)
    for row in range(CHUNK + 1):
        short[row * SIDE : (row + 1) * SIDE, :] = (hat_y[row : row + 1, :] * hat_z).astype(BF16)
    short[SHORT : SHORT + 16, :] = (hat_y * end_z).astype(BF16)
    for place, own in enumerate(owns):
        weighted[place * SIDE : (place + 1) * SIDE, :] = (own * hat_x).astype(BF16)
    ends = jnp.where(iota((16, LANES), 0).astype(F32) == row_of, end_x, 0.0)
    at = CHUNKS * 2 * SIDE
    weighted[at : at + 16, :] = ends.astype(BF16)


def add_deposit(short, weighted, total):
    product = lax.dot_general(
        short[...], weighted[...], (((1,), (1,)), ((), ())), preferred_element_type=F32
    )
    total[:, 0 : product.shape[1]] += product


def fill_cross(inbox, first, rows, cross):
    _, _, y, z = group_fields(inbox, first)
    end_y, end_z = end_hat(y), end_hat(z)
    end_y, end_z, end_both = keep(rows, [end_y, end_z, end_y * end_z])
    hat_y = hat(flat(inbox, first + 2, 4), SIDE)
    hat_z = hat(flat(inbox, first + 3, 4), SIDE)
    for row in range(SIDE):
        cross[row * SIDE : (row + 1) * SIDE, :] = (hat_y[row : row + 1, :] * hat_z).astype(BF16)
    cross[CELLS : CELLS + 32, :] = (end_y * hat_z).astype(BF16)
    cross[CELLS + 32 : CELLS + 64, :] = (hat_y * end_z).astype(BF16)
    last = jnp.where(iota((16, LANES), 0) == 0, end_both, 0.0)
    cross[CELLS + 64 : CELLS + 80, :] = last.astype(BF16)


def sample(inbox, first, rows, table, cross, kicks):
    mass, x, _, _ = group_fields(inbox, first)
    (end_x,) = keep(rows, [end_hat(x)])
    hat_x = hat(flat(inbox, first + 1, 4), SIDE)
    upper_level = flat(inbox, first, 4) < 0.0
    amount = table.shape[0] - 16
    depth = amount // 2
    sampled = jnp.dot(table[...], cross[...], preferred_element_type=F32)
    for axis in range(3):
        at = axis * SIDE
        picked = jnp.where(
            upper_level, sampled[depth + at : depth + at + SIDE, :], sampled[at : at + SIDE, :]
        )
        at = amount + axis
        far = jnp.where(upper_level, sampled[at + 3 : at + 4, :], sampled[at : at + 1, :])
        value = jnp.sum(hat_x * picked, axis=0, keepdims=True) + end_x * far
        for t in range(GROUP):
            kicks[pl.ds(first + (t * 4 + axis), 1), :] = value[:, t * 128 : (t + 1) * 128]


def spread_deposit(total, wide):
    wide[...] = jnp.zeros_like(wide)
    first, second = total[:, 0:128], total[:, 128:256]
    low = iota(first.shape, 1) < 2 * SIDE
    for place in range(CHUNKS):
        main = [first, pltpu.roll(first, 64, 1), second][place]
        ends = second if place == 0 else pltpu.roll(second, 128 - 2 * place, 1)
        both = jnp.where(low, main, ends)
        at = place * CHUNK * SIDE
        wide[at : at + SHORT, :] += both[0:SHORT, :]
        at = CELLS + SIDE + place * CHUNK
        wide[at : at + CHUNK + 1, :] += both[SHORT : SHORT + CHUNK + 1, :]


def kernel(
    devices,
    levels,
    count_ref,
    owner_ref,
    box_owner,
    mass_in,
    frac_in,
    cell_in,
    level_in,
    force_in,
    density,
    kick,
    outbox,
    inbox,
    kicks,
    returned,
    mass_ref,
    frac_ref,
    cell_ref,
    level_ref,
    force_ref,
    hots,
    force_out,
    force_spread,
    force_next,
    force_last,
    mass_out,
    mass_spread,
    mass_next,
    mass_last,
    force_middle,
    mass_middle,
    table,
    cross_a,
    cross_b,
    short_a,
    short_b,
    weighted_a,
    weighted_b,
    rows_a,
    rows_b,
    rows_c,
    rows_d,
    picks_back,
    total,
    wide,
    own_sem,
    tile_send,
    tile_recv,
    kick_send,
    kick_recv,
    load_sem,
    rim_sems,
):
    me = lax.axis_index("boxes")
    depth = 3 * SIDE
    rows = levels * depth
    groups = devices // INNER
    my_row = me // INNER
    pairs = groups // 2

    loads = [
        pltpu.make_async_copy(source, target, load_sem.at[place])
        for place, (source, target) in enumerate(
            [
                (mass_in, mass_ref),
                (frac_in, frac_ref),
                (cell_in, cell_ref),
                (level_in, level_ref),
                (force_in, force_ref),
            ]
        )
    ]
    for load in loads:
        load.start()
    barrier = pltpu.get_barrier_semaphore()
    each(
        devices,
        lambda step: pl.semaphore_signal(
            barrier, inc=1, device_id=(lax.rem(me + step, devices),), device_id_type=MESH
        ),
    )

    picks = slot_picks(owner_ref, count_ref[0], True)
    for load in loads[:4]:
        load.wait()
    cell = cell_ref[...]
    digits = [cell // CELLS, cell // SIDE % SIDE, cell % SIDE]
    fields = [jnp.where(level_ref[...] == 0, mass_ref[...], -mass_ref[...])]
    for axis in range(3):
        fields.append(digits[axis].astype(F32) + frac_ref[axis])
    packed = exact_dot(picks, jnp.concatenate(fields, axis=1))
    for order in range(2):
        for field in range(4):
            part = packed[order * devices : (order + 1) * devices, field * 128 : field * 128 + 128]
            outbox[pl.ds(order * 4 + field, devices, stride=8), :] = part

    loads[4].wait()
    force = force_ref[...]
    edges = jnp.dot(force, plane_pick(BF16, False), preferred_element_type=F32)
    fronts = []
    for place in range(levels * 3):
        at = place * SIDE
        front = force_ref[at : at + 16, :].astype(F32)[0:1, :]
        fronts.append(jnp.concatenate([front, edges[at : at + 1, :]], axis=1))
    values = pack_rims(edges, fronts)
    values = jnp.concatenate([values, jnp.zeros((256 - values.shape[0], 128), F32)], axis=0)
    for half in range(2):
        block = jnp.transpose(values[half * 128 : half * 128 + 128, :])
        force_out[:, :, half, :] = block.reshape(devices // INNER, INNER, 128)
    pl.semaphore_wait(barrier, devices - 1)

    force_hops = [
        rim_hops(force_out, force_middle.at[0], force_spread, rim_sems.at[0], devices, me),
        rim_hops(force_next, force_middle.at[1], force_last, rim_sems.at[1], devices, me),
    ]
    mass_hops = [
        rim_hops(mass_out, mass_middle.at[0], mass_spread, rim_sems.at[2], devices, me),
        rim_hops(mass_next, mass_middle.at[1], mass_last, rim_sems.at[3], devices, me),
    ]

    def tile_copy(hop, peer):
        return block_copy(outbox, inbox, tile_send, tile_recv.at[hop], peer, me)

    def send_tiles(hop):
        target = lax.rem(my_row + hop, groups) * INNER
        each(INNER, lambda step: tile_copy(hop, target + lax.rem(me + step, INNER)).start())

        @pl.when(hop > 0)
        def _():
            tile_copy(hop, target + lax.rem(me, INNER)).start()

    force_hops[0][0]()
    send_tiles(0)
    each(groups, send_tiles)
    own = pltpu.make_async_copy(outbox.at[block_rows(me)], inbox.at[block_rows(me)], own_sem)
    own.start()
    force_hops[0][1]()

    for level in range(levels):
        ways = rim_sources(box_owner, level, devices)
        for way in range(2):
            hots[pl.ds((way * levels + level) * 7 * devices, 7 * devices), :] = ways[way]
    picks_back[...] = slot_picks(owner_ref, count_ref[0], False)
    table[0:rows, 0:CELLS] = force
    blank = jnp.zeros((WIDE - CELLS - 80, LANES), BF16)
    cross_a[CELLS + 80 : WIDE, :] = blank
    cross_b[CELLS + 80 : WIDE, :] = blank
    total[...] = jnp.zeros_like(total)
    kicks[...] = jnp.zeros_like(kicks)

    def force_relay():
        force_hops[0][2]()
        values = jnp.concatenate(
            [force_spread[:, :, half, :].reshape(devices, 128) for half in range(2)], axis=1
        )
        chosen = choose(hots[0 : levels * 7 * devices, :], values.astype(BF16), 3, devices)
        for half in range(2):
            block = chosen[:, half * 128 : half * 128 + 128]
            force_next[:, :, half, :] = block.reshape(devices // INNER, INNER, 128)
        force_hops[1][0]()

    def mass_relay():
        mass_hops[0][2]()
        values = mass_spread[:, :, 0, :].reshape(devices, 128)
        high = values.astype(BF16)
        rest = (values - high.astype(F32)).astype(BF16)
        way = hots[levels * 7 * devices : 2 * levels * 7 * devices, :]
        chosen = choose(way, jnp.concatenate([high, rest], axis=1), 1, devices)
        chosen = chosen[:, 0:128] + chosen[:, 128:256]
        mass_next[:, :, 0, :] = chosen.reshape(devices // INNER, INNER, 128)
        mass_hops[1][0]()

    def stages(pair, at, acts):
        for place, act in zip(at, acts):
            pl.when(pair == place)(act)

    def await_group(hop):
        amount = devices // groups * 8
        if isinstance(hop, int) and hop == 0:
            own.wait()
            amount -= 8
        pltpu.make_async_remote_copy(
            src_ref=outbox.at[pl.ds(0, amount)],
            dst_ref=inbox.at[pl.ds(0, amount)],
            send_sem=tile_send,
            recv_sem=tile_recv.at[hop],
            device_id=(lax.rem(me + 1, devices),),
            device_id_type=MESH,
        ).wait_recv()

    def first_of(hop):
        return pl.multiple_of(lax.rem(my_row + groups - hop, groups) * (INNER * 8), 8)

    def fill_a(hop):
        fill_deposit(inbox, first_of(hop), rows_a, short_a, weighted_a)

    def fill_b(hop):
        fill_deposit(inbox, first_of(hop), rows_b, short_b, weighted_b)

    await_group(0)
    fill_a(0)

    def deposit_pair(pair, carry):
        stages(pair, FORCE_STAGES, (force_relay, force_hops[1][1]))
        await_group(2 * pair + 1)
        await_group(2 * pair + 2)
        fill_b(2 * pair + 1)
        add_deposit(short_a, weighted_a, total)
        fill_a(2 * pair + 2)
        add_deposit(short_b, weighted_b, total)
        return carry

    lax.fori_loop(0, pairs - 1, deposit_pair, 0)
    await_group(groups - 1)
    fill_b(groups - 1)
    add_deposit(short_a, weighted_a, total)
    add_deposit(short_b, weighted_b, total)

    spread_deposit(total, wide)
    flipped = jnp.transpose(wide[...])
    density[...] = flipped[0 : levels * SIDE, 0:CELLS]
    beyond = flipped[levels * SIDE : levels * SIDE + levels, :]
    values = pack_rims(
        flipped[0 : levels * SIDE, CELLS:WIDE],
        [beyond[level : level + 1, :] for level in range(levels)],
    )
    values = jnp.concatenate([values, jnp.zeros((128 - values.shape[0], 128), F32)], axis=0)
    mass_out[:, :, 0, :] = jnp.transpose(values).reshape(devices // INNER, INNER, 128)
    mass_hops[0][0]()

    force_hops[1][2]()
    values = jnp.concatenate(
        [jnp.transpose(force_last[:, :, half, :].reshape(devices, 128)) for half in range(2)],
        axis=0,
    )
    edges, fronts = unpack_rims(values, levels * 3)
    table[0:rows, CELLS:WIDE] = edges.astype(BF16)
    fronts.append(jnp.zeros((16 - len(fronts), WIDE), F32))
    table[rows : rows + 16, :] = jnp.concatenate(fronts, axis=0).astype(BF16)

    def kick_copy(peer):
        return block_copy(kicks, returned, kick_send, kick_recv, peer, me)

    def send_kicks(hop):
        target = lax.rem(my_row + groups - hop, groups) * INNER
        for place in range(INNER):
            kick_copy(target + place).start()

    def cross_a_of(hop):
        fill_cross(inbox, first_of(hop), rows_a, cross_a)

    def cross_b_of(hop):
        fill_cross(inbox, first_of(hop), rows_b, cross_b)

    def sample_a_of(hop):
        sample(inbox, first_of(hop), rows_c, table, cross_a, kicks)

    def sample_b_of(hop):
        sample(inbox, first_of(hop), rows_d, table, cross_b, kicks)

    cross_a_of(1)

    def sample_pair(pair, carry):
        stages(pair, MASS_STAGES, (mass_hops[0][1], mass_relay, mass_hops[1][1]))
        cross_b_of(2 * pair + 2)
        sample_a_of(2 * pair + 1)
        cross_a_of(2 * pair + 3)
        sample_b_of(2 * pair + 2)
        send_kicks(2 * pair + 1)
        send_kicks(2 * pair + 2)
        return carry

    lax.fori_loop(0, pairs - 1, sample_pair, 0)
    cross_b_of(0)
    sample_a_of(groups - 1)
    send_kicks(groups - 1)
    sample_b_of(0)
    each(INNER, lambda step: kick_copy(my_row * INNER + lax.rem(me + step, INNER)).start())
    kept = pltpu.make_async_copy(kicks.at[block_rows(me)], returned.at[block_rows(me)], own_sem)
    kept.start()

    mass_hops[1][2]()
    values = jnp.transpose(mass_last[:, :, 0, :].reshape(devices, 128))
    edges, fronts = unpack_rims(values, levels)
    first_row = iota((SIDE, 1), 0) == 0
    low = [
        edges[level * SIDE : (level + 1) * SIDE, :]
        + jnp.where(first_row, fronts[level][:, CELLS:WIDE], 0.0)
        for level in range(levels)
    ]
    low = jnp.concatenate(low, axis=0)
    high = low.astype(BF16)
    pair = jnp.concatenate([high, (low - high.astype(F32)).astype(BF16)], axis=0)
    added = jnp.dot(pair, plane_pick(BF16, True), preferred_element_type=F32)
    added = added[0 : levels * SIDE, :] + added[levels * SIDE : 2 * levels * SIDE, :]
    for level in range(levels):
        at = slice(level * SIDE, (level + 1) * SIDE)
        density[at, :] += added[at, :] + jnp.where(first_row, fronts[level][:, 0:CELLS], 0.0)

    all_blocks(outbox, inbox, tile_send, tile_recv.at[0], devices, me).wait_send()
    kept.wait()
    all_blocks(kicks, returned, kick_send, kick_recv, devices, me).wait()
    parts = []
    for order in range(2):
        columns = [returned[pl.ds(order * 4 + axis, devices, stride=8), :] for axis in range(3)]
        parts.append(jnp.concatenate(columns, axis=1))
    mine = exact_dot(picks_back[...], jnp.concatenate(parts, axis=0))
    for axis in range(3):
        kick[axis] = mine[:, axis * 128 : (axis + 1) * 128]


def on_device(
    tile_mass, tile_frac, tile_cell, tile_level, tile_owner, tile_count, box_owner, force_field
):
    devices = lax.axis_size("boxes")
    levels = box_owner.shape[0]
    tiles, width = tile_mass.shape
    rows = levels * 3 * SIDE
    shape = jax.ShapeDtypeStruct
    vmem = pl.BlockSpec(memory_space=pltpu.VMEM)
    smem = pl.BlockSpec(memory_space=pltpu.SMEM)
    dma = pltpu.SemaphoreType.DMA
    blocks = pltpu.VMEM((devices * 8, width), F32)
    spread_rows = CHUNKS * 2 * SIDE + 16
    density, kick = pl.pallas_call(
        functools.partial(kernel, devices, levels),
        out_shape=(shape((levels * SIDE, CELLS), F32), shape((3, tiles, width), F32)),
        in_specs=[smem, vmem, vmem] + [pl.BlockSpec(memory_space=pl.ANY)] * 5,
        out_specs=(vmem, vmem),
        scratch_shapes=[
            blocks,
            blocks,
            blocks,
            blocks,
            pltpu.VMEM((tiles, width), F32),
            pltpu.VMEM((3, tiles, width), F32),
            pltpu.VMEM((tiles, width), jnp.int32),
            pltpu.VMEM((tiles, width), jnp.int32),
            pltpu.VMEM((rows, CELLS), BF16),
            pltpu.VMEM((2 * levels * 7 * devices, devices), BF16),
        ]
        + [pltpu.VMEM((devices // INNER, INNER, 2, 128), F32)] * 4
        + [pltpu.VMEM((devices // INNER, INNER, 1, 128), F32)] * 4
        + [
            pltpu.VMEM((2, INNER, devices // INNER, 2, 128), F32),
            pltpu.VMEM((2, INNER, devices // INNER, 1, 128), F32),
        ]
        + [
            pltpu.VMEM((rows + 16, WIDE), BF16),
            pltpu.VMEM((WIDE, LANES), BF16),
            pltpu.VMEM((WIDE, LANES), BF16),
            pltpu.VMEM((SHORT + 16, LANES), BF16),
            pltpu.VMEM((SHORT + 16, LANES), BF16),
            pltpu.VMEM((spread_rows, LANES), BF16),
            pltpu.VMEM((spread_rows, LANES), BF16),
            pltpu.VMEM((10 * GROUP, 128), F32),
            pltpu.VMEM((10 * GROUP, 128), F32),
            pltpu.VMEM((GROUP, 128), F32),
            pltpu.VMEM((GROUP, 128), F32),
            pltpu.VMEM((tiles, 2 * devices), BF16),
            pltpu.VMEM((SHORT + 16, 256), F32),
            pltpu.VMEM((WIDE, 128), F32),
            dma,
            dma,
            dma((devices // INNER,)),
            dma,
            dma,
            dma((5,)),
            dma((4, 4)),
        ],
        compiler_params=pltpu.CompilerParams(
            collective_id=0, has_side_effects=True, vmem_limit_bytes=60 << 20
        ),
        name="deposit_and_sample",
    )(
        tile_count,
        tile_owner.reshape(1, tiles),
        box_owner,
        tile_mass,
        jnp.transpose(tile_frac, (1, 0, 2)),
        tile_cell,
        tile_level,
        force_field.reshape(rows, CELLS),
    )
    return (density.reshape(levels, SIDE, CELLS), jnp.transpose(kick, (1, 0, 2)))


def solution(mesh):
    in_specs = (
        P("boxes", None),
        P("boxes", None, None),
        P("boxes", None),
        P("boxes", None),
        P("boxes", None),
        P("boxes"),
        P(),
        P(None, None, "boxes", None),
    )
    out_specs = (P(None, "boxes", None), P("boxes", None, None))
    return jax.shard_map(
        on_device, mesh=mesh, in_specs=in_specs, out_specs=out_specs, check_vma=False
    )
```

```python
import functools

import jax
import jax.numpy as jnp
import numpy as np
from jax import lax
from jax.experimental import pallas as pl
from jax.experimental.pallas import tpu as pltpu
from jax.sharding import PartitionSpec as P

MESH = pl.DeviceIdType.MESH
F32 = jnp.float32
BF16 = jnp.bfloat16
LAT_X = 4
LAT_Z = 4
SIDE = 32
CELLS = SIDE * SIDE
WIDE = CELLS + 128
INNER = 8
GROUP = 2 * INNER
LANES = GROUP * 128
CHUNK = 11
CHUNKS = 3
SHORT = (CHUNK + 1) * SIDE
FORCE_STAGE = 5
MASS_STAGES = (1, 3, 5)

direction_table = np.array(
    [[1, 0, 0], [0, 1, 0], [0, 0, 1], [1, 1, 0], [1, 0, 1], [0, 1, 1], [1, 1, 1]], dtype=np.int32
)


def iota(shape, dim):
    return lax.broadcasted_iota(jnp.int32, shape, dim)


def ones_at(mask, dtype):
    return jnp.where(mask, 1.0, 0.0).astype(dtype)


def exact_dot(picks, values):
    width = values.shape[1]
    high = values.astype(BF16)
    rest = values - high.astype(F32)
    middle = rest.astype(BF16)
    low = (rest - middle.astype(F32)).astype(BF16)
    parts = jnp.concatenate([high, middle, low], axis=1)
    found = jnp.dot(picks, parts, preferred_element_type=F32)
    return (found[:, 0:width] + found[:, width : 2 * width]) + found[:, 2 * width : 3 * width]


def kind_of(value, parts):
    slab = value // 8
    group = slab // 5
    part = slab % 5
    kind = jnp.where(part == 3, 5, part)
    corner = value % 8
    kind = jnp.where(part == 4, jnp.where(corner == 0, 3, jnp.where(corner == 1, 4, 6)), kind)
    return group // parts, kind


def pack_rims(edges, fronts):
    lane = iota((8, 128), 1)
    row = iota((8, 128), 0)
    slabs = []
    for place, front in enumerate(fronts):
        pieces = [front[:, 128 * part : 128 * part + 128] for part in range(8)]
        slabs.append(jnp.concatenate(pieces, axis=0))
        for start in (0, 32, 64):
            total = None
            for part in range(4):
                at = place * SIDE + part * 8
                moved = pltpu.roll(edges[at : at + 8, :], (32 * part - start) % 128, 1)
                total = moved if total is None else jnp.where(lane >= 32 * part, moved, total)
            slabs.append(total)
        last = jnp.broadcast_to(front[:, CELLS:WIDE], (8, 128))
        corners = jnp.where(row == 0, last, pltpu.roll(last, 96, 1))
        slabs.append(jnp.where(row == 2, pltpu.roll(last, 64, 1), corners))
    return jnp.concatenate(slabs, axis=0)


def unpack_rims(values, amount):
    lane = iota((8, 128), 1)
    edges, fronts = [], []
    for place in range(amount):
        at = place * 40
        pieces = [values[at + part : at + part + 1, :] for part in range(8)]
        plane_y, plane_z, line = [values[at + 8 * n : at + 8 * n + 8, :] for n in (1, 2, 3)]
        for part in range(4):
            moved = pltpu.roll(plane_z, (32 - 32 * part) % 128, 1)
            moved = jnp.where(lane < 32, pltpu.roll(plane_y, (-32 * part) % 128, 1), moved)
            moved = jnp.where(lane == 64, pltpu.roll(line, (64 - 32 * part) % 128, 1), moved)
            edges.append(jnp.where(lane <= 64, moved, 0.0))
        corners = values[at + 32 : at + 40, :]
        first = jnp.where(lane < 32, corners, 0.0)[0:1, :]
        second = jnp.where((lane >= 32) & (lane < 64), pltpu.roll(corners, 32, 1), 0.0)[1:2, :]
        third = jnp.where(lane == 64, pltpu.roll(corners, 64, 1), 0.0)[2:3, :]
        fronts.append(jnp.concatenate(pieces + [first + second + third], axis=1))
    return jnp.concatenate(edges, axis=0), fronts


def plane_pick(dtype, flip):
    shape = (128, CELLS) if flip else (CELLS, 128)
    lane = iota(shape, 0 if flip else 1)
    cell = iota(shape, 1 if flip else 0)
    wanted = jnp.where(lane < 32, lane, jnp.where(lane < 64, (lane - 32) * SIDE, -1))
    wanted = jnp.where(lane == 64, 0, wanted)
    return ones_at(cell == wanted, dtype)


def slot_picks(owner_ref, count, by_slot):
    tiles = owner_ref.shape[1]
    across = jnp.broadcast_to(owner_ref[...], (tiles, tiles))
    down = jnp.transpose(across)
    same = across == down
    first, second = iota((tiles, tiles), 0), iota((tiles, tiles), 1)
    if by_slot:
        earlier = jnp.where(same & (first < second), 1.0, 0.0)
        rank = jnp.sum(earlier, axis=0, keepdims=True)
        fits = (across == first) & (second < count)
    else:
        earlier = jnp.where(same & (second < first), 1.0, 0.0)
        rank = jnp.sum(earlier, axis=1, keepdims=True)
        fits = (down == second) & (first < count)
    picks = [jnp.where(fits & (rank == float(order)), 1.0, 0.0) for order in range(2)]
    return jnp.concatenate(picks, axis=0 if by_slot else 1).astype(BF16)


def rim_sources(box_owner, level, devices):
    lat_y = devices // (LAT_X * LAT_Z)
    square = (devices, devices)
    across = jnp.broadcast_to(box_owner[level : level + 1, :], square)
    down = jnp.transpose(across).astype(F32).astype(BF16)
    hot = ones_at(across == iota(square, 0), BF16)
    places = iota(square, 0).astype(F32).astype(BF16)
    box = jnp.dot(hot, places, preferred_element_type=F32).astype(jnp.int32)
    at = [box // (lat_y * LAT_Z), box // LAT_Z % lat_y, box % LAT_Z]
    found = []
    for sign in (1, -1):
        hots = []
        for step in direction_table:
            near = [
                (at[axis] + (sign * int(step[axis]) + extent)) % extent
                for axis, extent in enumerate((LAT_X, lat_y, LAT_Z))
            ]
            wanted = (near[0] * lat_y + near[1]) * LAT_Z + near[2]
            hots.append(ones_at(wanted == iota(square, 1), BF16))
        owners = jnp.dot(jnp.concatenate(hots, axis=0), down, preferred_element_type=F32)
        found.append(ones_at(owners == iota(owners.shape, 1).astype(F32), BF16))
    return found


def choose(hots, values, parts, devices):
    levels = hots.shape[0] // (7 * devices)
    width = values.shape[1]
    level_of, kind = kind_of(iota((1, width), 1) % (128 if parts == 1 else 256), parts)
    total = jnp.zeros((devices, width), F32)
    for level in range(levels):
        at = level * 7 * devices
        found = jnp.dot(hots[at : at + 7 * devices, :], values, preferred_element_type=F32)
        for direction in range(7):
            part = found[direction * devices : (direction + 1) * devices, :]
            total = jnp.where((level_of == level) & (kind == direction), part, total)
    return total


def each(count, act):
    def body(step, carry):
        act(step)
        return carry

    lax.fori_loop(1, count, body, 0)


def block_rows(device):
    return pl.ds(pl.multiple_of(device * 8, 8), 8)


def block_copy(source, target, send, recv, peer, me):
    return pltpu.make_async_remote_copy(
        src_ref=source.at[block_rows(peer)],
        dst_ref=target.at[block_rows(me)],
        send_sem=send,
        recv_sem=recv,
        device_id=(peer,),
        device_id_type=MESH,
    )


def all_blocks(source, target, send, recv, devices, me):
    rows = (devices - 1) * 8
    return pltpu.make_async_remote_copy(
        src_ref=source.at[pl.ds(0, rows)],
        dst_ref=target.at[pl.ds(0, rows)],
        send_sem=send,
        recv_sem=recv,
        device_id=(lax.rem(me + 1, devices),),
        device_id_type=MESH,
    )


def rim_hops(source, middle, target, sems, devices, me):
    rows = devices // INNER
    row, place = me // INNER, lax.rem(me, INNER)

    def first(step):
        other = lax.rem(place + step, INNER)
        return pltpu.make_async_remote_copy(
            src_ref=source.at[:, other],
            dst_ref=middle.at[place],
            send_sem=sems.at[0],
            recv_sem=sems.at[1],
            device_id=(row * INNER + other,),
            device_id_type=MESH,
        )

    def second(step):
        other = lax.rem(row + step, rows)
        return pltpu.make_async_remote_copy(
            src_ref=middle.at[:, other],
            dst_ref=target.at[row],
            send_sem=sems.at[2],
            recv_sem=sems.at[3],
            device_id=(other * INNER + place,),
            device_id_type=MESH,
        )

    def start():
        each(INNER, lambda step: first(step).start())
        middle[place] = source[:, place]

    def forward():
        pltpu.make_async_remote_copy(
            src_ref=middle.at[pl.ds(0, INNER - 1)],
            dst_ref=middle.at[pl.ds(0, INNER - 1)],
            send_sem=sems.at[0],
            recv_sem=sems.at[1],
            device_id=(row * INNER + lax.rem(place + 1, INNER),),
            device_id_type=MESH,
        ).wait()
        each(rows, lambda step: second(step).start())
        target[row] = middle[:, row]

    def finish():
        pltpu.make_async_remote_copy(
            src_ref=target.at[pl.ds(0, rows - 1)],
            dst_ref=target.at[pl.ds(0, rows - 1)],
            send_sem=sems.at[2],
            recv_sem=sems.at[3],
            device_id=(lax.rem(row + 1, rows) * INNER + place,),
            device_id_type=MESH,
        ).wait()

    return start, forward, finish


def rim_copy(source, target, sems, peer, me):
    return pltpu.make_async_remote_copy(
        src_ref=source.at[peer],
        dst_ref=target.at[me],
        send_sem=sems.at[0],
        recv_sem=sems.at[1],
        device_id=(peer,),
        device_id_type=MESH,
    )


def all_rims(source, target, sems, devices, me):
    return pltpu.make_async_remote_copy(
        src_ref=source.at[pl.ds(0, devices - 1)],
        dst_ref=target.at[pl.ds(0, devices - 1)],
        send_sem=sems.at[0],
        recv_sem=sems.at[1],
        device_id=(lax.rem(me + 1, devices),),
        device_id_type=MESH,
    )


def hat(coord, rows):
    ids = iota((rows, coord.shape[1]), 0).astype(F32)
    return jnp.maximum(0.0, 1.0 - jnp.abs(coord - ids))


def group_fields(inbox, first):
    return [inbox[pl.ds(first + field, GROUP, stride=4), :] for field in range(4)]


def flat(ref, first, stride):
    return jnp.concatenate([ref[pl.ds(first + t * stride, 1), :] for t in range(GROUP)], axis=1)


def end_hat(coord):
    return jnp.maximum(0.0, 1.0 - jnp.abs(coord - float(SIDE)))


def keep(rows, values):
    for place, value in enumerate(values):
        rows[place * GROUP : (place + 1) * GROUP, :] = value
    return [flat(rows, place * GROUP, 1) for place in range(len(values))]


def fill_deposit(inbox, first, rows, short, weighted):
    mass, x, y, z = group_fields(inbox, first)
    chunk = jnp.where(y >= 2.0 * CHUNK, 2.0, jnp.where(y >= CHUNK, 1.0, 0.0))
    row_of = 2.0 * chunk + jnp.where(mass < 0.0, 1.0, 0.0)
    size = jnp.abs(mass)
    owns = [jnp.where(row_of == float(place), size, 0.0) for place in range(CHUNKS * 2)]
    rest = [y - chunk * CHUNK, end_hat(z), row_of, size * end_hat(x)]
    *owns, near_y, end_z, row_of, end_x = keep(rows, owns + rest)
    hat_x = hat(flat(inbox, first + 1, 4), SIDE)
    hat_y = hat(near_y, 16)
    hat_z = hat(flat(inbox, first + 3, 4), SIDE)
    for row in range(CHUNK + 1):
        short[row * SIDE : (row + 1) * SIDE, :] = (hat_y[row : row + 1, :] * hat_z).astype(BF16)
    short[SHORT : SHORT + 16, :] = (hat_y * end_z).astype(BF16)
    for place, own in enumerate(owns):
        weighted[place * SIDE : (place + 1) * SIDE, :] = (own * hat_x).astype(BF16)
    ends = jnp.where(iota((16, LANES), 0).astype(F32) == row_of, end_x, 0.0)
    at = CHUNKS * 2 * SIDE
    weighted[at : at + 16, :] = ends.astype(BF16)


def add_deposit(short, weighted, total):
    product = lax.dot_general(
        short[...], weighted[...], (((1,), (1,)), ((), ())), preferred_element_type=F32
    )
    total[:, 0 : product.shape[1]] += product


def fill_cross(inbox, first, rows, cross):
    _, _, y, z = group_fields(inbox, first)
    end_y, end_z = end_hat(y), end_hat(z)
    end_y, end_z, end_both = keep(rows, [end_y, end_z, end_y * end_z])
    hat_y = hat(flat(inbox, first + 2, 4), SIDE)
    hat_z = hat(flat(inbox, first + 3, 4), SIDE)
    for row in range(SIDE):
        cross[row * SIDE : (row + 1) * SIDE, :] = (hat_y[row : row + 1, :] * hat_z).astype(BF16)
    cross[CELLS : CELLS + 32, :] = (end_y * hat_z).astype(BF16)
    cross[CELLS + 32 : CELLS + 64, :] = (hat_y * end_z).astype(BF16)
    last = jnp.where(iota((16, LANES), 0) == 0, end_both, 0.0)
    cross[CELLS + 64 : CELLS + 80, :] = last.astype(BF16)


def sample(inbox, first, rows, table, cross, kicks):
    mass, x, _, _ = group_fields(inbox, first)
    (end_x,) = keep(rows, [end_hat(x)])
    hat_x = hat(flat(inbox, first + 1, 4), SIDE)
    upper_level = flat(inbox, first, 4) < 0.0
    amount = table.shape[0] - 16
    depth = amount // 2
    sampled = jnp.dot(table[...], cross[...], preferred_element_type=F32)
    for axis in range(3):
        at = axis * SIDE
        picked = jnp.where(
            upper_level, sampled[depth + at : depth + at + SIDE, :], sampled[at : at + SIDE, :]
        )
        at = amount + axis
        far = jnp.where(upper_level, sampled[at + 3 : at + 4, :], sampled[at : at + 1, :])
        value = jnp.sum(hat_x * picked, axis=0, keepdims=True) + end_x * far
        for t in range(GROUP):
            kicks[pl.ds(first + (t * 4 + axis), 1), :] = value[:, t * 128 : (t + 1) * 128]


def spread_deposit(total, wide):
    wide[...] = jnp.zeros_like(wide)
    first, second = total[:, 0:128], total[:, 128:256]
    low = iota(first.shape, 1) < 2 * SIDE
    for place in range(CHUNKS):
        main = [first, pltpu.roll(first, 64, 1), second][place]
        ends = second if place == 0 else pltpu.roll(second, 128 - 2 * place, 1)
        both = jnp.where(low, main, ends)
        at = place * CHUNK * SIDE
        wide[at : at + SHORT, :] += both[0:SHORT, :]
        at = CELLS + SIDE + place * CHUNK
        wide[at : at + CHUNK + 1, :] += both[SHORT : SHORT + CHUNK + 1, :]


def kernel(
    devices,
    levels,
    count_ref,
    owner_in,
    box_in,
    mass_in,
    frac_in,
    cell_in,
    level_in,
    force_in,
    density,
    kick,
    outbox,
    inbox,
    kicks,
    returned,
    owner_ref,
    box_owner,
    mass_ref,
    frac_ref,
    cell_ref,
    level_ref,
    force_ref,
    hots,
    force_out,
    force_spread,
    force_next,
    force_last,
    mass_out,
    mass_spread,
    mass_next,
    mass_last,
    force_middle,
    mass_middle,
    table,
    cross_a,
    cross_b,
    short_a,
    short_b,
    weighted_a,
    weighted_b,
    rows_a,
    rows_b,
    rows_c,
    rows_d,
    picks_back,
    total,
    wide,
    own_sem,
    tile_send,
    tile_recv,
    kick_send,
    kick_recv,
    load_sem,
    rim_sems,
):
    me = lax.axis_index("boxes")
    depth = 3 * SIDE
    rows = levels * depth
    groups = devices // INNER
    my_row = me // INNER
    pairs = groups // 2

    loads = [
        pltpu.make_async_copy(source, target, load_sem.at[place])
        for place, (source, target) in enumerate(
            [
                (owner_in, owner_ref),
                (mass_in, mass_ref),
                (frac_in, frac_ref),
                (cell_in, cell_ref),
                (level_in, level_ref),
                (force_in, force_ref),
                (box_in, box_owner),
            ]
        )
    ]
    for load in loads:
        load.start()
    barrier = pltpu.get_barrier_semaphore()
    each(
        devices,
        lambda step: pl.semaphore_signal(
            barrier, inc=1, device_id=(lax.rem(me + step, devices),), device_id_type=MESH
        ),
    )

    loads[0].wait()
    picks = slot_picks(owner_ref, count_ref[0], True)
    for load in loads[1:5]:
        load.wait()
    cell = cell_ref[...]
    digits = [cell // CELLS, cell // SIDE % SIDE, cell % SIDE]
    fields = [jnp.where(level_ref[...] == 0, mass_ref[...], -mass_ref[...])]
    for axis in range(3):
        fields.append(digits[axis].astype(F32) + frac_ref[axis])
    packed = exact_dot(picks, jnp.concatenate(fields, axis=1))
    for order in range(2):
        for field in range(4):
            part = packed[order * devices : (order + 1) * devices, field * 128 : field * 128 + 128]
            outbox[pl.ds(order * 4 + field, devices, stride=8), :] = part

    loads[5].wait()
    loads[6].wait()
    force = force_ref[...]
    edges = jnp.dot(force, plane_pick(BF16, False), preferred_element_type=F32)
    fronts = []
    for place in range(levels * 3):
        at = place * SIDE
        front = force_ref[at : at + 16, :].astype(F32)[0:1, :]
        fronts.append(jnp.concatenate([front, edges[at : at + 1, :]], axis=1))
    values = pack_rims(edges, fronts)
    values = jnp.concatenate([values, jnp.zeros((256 - values.shape[0], 128), F32)], axis=0)
    for half in range(2):
        block = jnp.transpose(values[half * 128 : half * 128 + 128, :])
        force_out[:, :, half, :] = block.reshape(devices // INNER, INNER, 128)
    pl.semaphore_wait(barrier, devices - 1)

    force_hops = rim_hops(force_out, force_middle, force_spread, rim_sems.at[0], devices, me)
    mass_hops = [
        rim_hops(mass_out, mass_middle.at[0], mass_spread, rim_sems.at[2], devices, me),
        rim_hops(mass_next, mass_middle.at[1], mass_last, rim_sems.at[3], devices, me),
    ]

    def tile_copy(hop, peer):
        return block_copy(outbox, inbox, tile_send, tile_recv.at[hop], peer, me)

    def send_tiles(hop):
        target = lax.rem(my_row + hop, groups) * INNER
        each(INNER, lambda step: tile_copy(hop, target + lax.rem(me + step, INNER)).start())

        @pl.when(hop > 0)
        def _():
            tile_copy(hop, target + lax.rem(me, INNER)).start()

    force_hops[0]()
    send_tiles(0)
    each(groups, send_tiles)
    own = pltpu.make_async_copy(outbox.at[block_rows(me)], inbox.at[block_rows(me)], own_sem)
    own.start()
    force_hops[1]()

    for level in range(levels):
        ways = rim_sources(box_owner, level, devices)
        for way in range(2):
            hots[pl.ds((way * levels + level) * 7 * devices, 7 * devices), :] = ways[way]
    picks_back[...] = slot_picks(owner_ref, count_ref[0], False)
    table[0:rows, 0:CELLS] = force
    blank = jnp.zeros((WIDE - CELLS - 80, LANES), BF16)
    cross_a[CELLS + 80 : WIDE, :] = blank
    cross_b[CELLS + 80 : WIDE, :] = blank
    total[...] = jnp.zeros_like(total)
    kicks[...] = jnp.zeros_like(kicks)

    def force_relay():
        force_hops[2]()
        values = jnp.concatenate(
            [force_spread[:, :, half, :].reshape(devices, 128) for half in range(2)], axis=1
        )
        chosen = choose(hots[0 : levels * 7 * devices, :], values.astype(BF16), 3, devices)
        for half in range(2):
            force_next[:, half, :] = chosen[:, half * 128 : half * 128 + 128]
        each(
            devices,
            lambda step: rim_copy(
                force_next, force_last, rim_sems.at[1], lax.rem(me + step, devices), me
            ).start(),
        )
        force_last[me] = force_next[me]

    def mass_relay():
        mass_hops[0][2]()
        values = mass_spread[:, :, 0, :].reshape(devices, 128)
        high = values.astype(BF16)
        rest = (values - high.astype(F32)).astype(BF16)
        way = hots[levels * 7 * devices : 2 * levels * 7 * devices, :]
        chosen = choose(way, jnp.concatenate([high, rest], axis=1), 1, devices)
        chosen = chosen[:, 0:128] + chosen[:, 128:256]
        mass_next[:, :, 0, :] = chosen.reshape(devices // INNER, INNER, 128)
        mass_hops[1][0]()

    def stages(pair, at, acts):
        for place, act in zip(at, acts):
            pl.when(pair == place)(act)

    def await_group(hop):
        amount = devices // groups * 8
        if isinstance(hop, int) and hop == 0:
            own.wait()
            amount -= 8
        pltpu.make_async_remote_copy(
            src_ref=outbox.at[pl.ds(0, amount)],
            dst_ref=inbox.at[pl.ds(0, amount)],
            send_sem=tile_send,
            recv_sem=tile_recv.at[hop],
            device_id=(lax.rem(me + 1, devices),),
            device_id_type=MESH,
        ).wait_recv()

    def first_of(hop):
        return pl.multiple_of(lax.rem(my_row + groups - hop, groups) * (INNER * 8), 8)

    def fill_a(hop):
        fill_deposit(inbox, first_of(hop), rows_a, short_a, weighted_a)

    def fill_b(hop):
        fill_deposit(inbox, first_of(hop), rows_b, short_b, weighted_b)

    await_group(0)
    fill_a(0)

    def deposit_pair(pair, carry):
        pl.when(pair == FORCE_STAGE)(force_relay)
        await_group(2 * pair + 1)
        await_group(2 * pair + 2)
        fill_b(2 * pair + 1)
        add_deposit(short_a, weighted_a, total)
        fill_a(2 * pair + 2)
        add_deposit(short_b, weighted_b, total)
        return carry

    lax.fori_loop(0, pairs - 1, deposit_pair, 0)
    await_group(groups - 1)
    fill_b(groups - 1)
    add_deposit(short_a, weighted_a, total)
    add_deposit(short_b, weighted_b, total)

    spread_deposit(total, wide)
    flipped = jnp.transpose(wide[...])
    density[...] = flipped[0 : levels * SIDE, 0:CELLS]
    beyond = flipped[levels * SIDE : levels * SIDE + levels, :]
    values = pack_rims(
        flipped[0 : levels * SIDE, CELLS:WIDE],
        [beyond[level : level + 1, :] for level in range(levels)],
    )
    values = jnp.concatenate([values, jnp.zeros((128 - values.shape[0], 128), F32)], axis=0)
    mass_out[:, :, 0, :] = jnp.transpose(values).reshape(devices // INNER, INNER, 128)
    mass_hops[0][0]()

    def kick_copy(peer):
        return block_copy(kicks, returned, kick_send, kick_recv, peer, me)

    def send_kicks(hop):
        target = lax.rem(my_row + groups - hop, groups) * INNER
        for place in range(INNER):
            kick_copy(target + place).start()

    def cross_a_of(hop):
        fill_cross(inbox, first_of(hop), rows_a, cross_a)

    def cross_b_of(hop):
        fill_cross(inbox, first_of(hop), rows_b, cross_b)

    def sample_a_of(hop):
        sample(inbox, first_of(hop), rows_c, table, cross_a, kicks)

    def sample_b_of(hop):
        sample(inbox, first_of(hop), rows_d, table, cross_b, kicks)

    cross_a_of(1)

    all_rims(force_next, force_last, rim_sems.at[1], devices, me).wait()
    values = jnp.concatenate(
        [jnp.transpose(force_last[:, half, :]) for half in range(2)], axis=0
    )
    edges, fronts = unpack_rims(values, levels * 3)
    table[0:rows, CELLS:WIDE] = edges.astype(BF16)
    fronts.append(jnp.zeros((16 - len(fronts), WIDE), F32))
    table[rows : rows + 16, :] = jnp.concatenate(fronts, axis=0).astype(BF16)

    def sample_pair(pair, carry):
        stages(pair, MASS_STAGES, (mass_hops[0][1], mass_relay, mass_hops[1][1]))
        cross_b_of(2 * pair + 2)
        sample_a_of(2 * pair + 1)
        cross_a_of(2 * pair + 3)
        sample_b_of(2 * pair + 2)
        send_kicks(2 * pair + 1)
        send_kicks(2 * pair + 2)
        return carry

    lax.fori_loop(0, pairs - 1, sample_pair, 0)
    cross_b_of(0)
    sample_a_of(groups - 1)
    send_kicks(groups - 1)
    sample_b_of(0)
    each(INNER, lambda step: kick_copy(my_row * INNER + lax.rem(me + step, INNER)).start())
    kept = pltpu.make_async_copy(kicks.at[block_rows(me)], returned.at[block_rows(me)], own_sem)
    kept.start()

    mass_hops[1][2]()
    values = jnp.transpose(mass_last[:, :, 0, :].reshape(devices, 128))
    edges, fronts = unpack_rims(values, levels)
    first_row = iota((SIDE, 1), 0) == 0
    low = [
        edges[level * SIDE : (level + 1) * SIDE, :]
        + jnp.where(first_row, fronts[level][:, CELLS:WIDE], 0.0)
        for level in range(levels)
    ]
    low = jnp.concatenate(low, axis=0)
    high = low.astype(BF16)
    pair = jnp.concatenate([high, (low - high.astype(F32)).astype(BF16)], axis=0)
    added = jnp.dot(pair, plane_pick(BF16, True), preferred_element_type=F32)
    added = added[0 : levels * SIDE, :] + added[levels * SIDE : 2 * levels * SIDE, :]
    for level in range(levels):
        at = slice(level * SIDE, (level + 1) * SIDE)
        density[at, :] += added[at, :] + jnp.where(first_row, fronts[level][:, 0:CELLS], 0.0)

    all_blocks(outbox, inbox, tile_send, tile_recv.at[0], devices, me).wait_send()
    kept.wait()
    all_blocks(kicks, returned, kick_send, kick_recv, devices, me).wait()
    parts = []
    for order in range(2):
        columns = [returned[pl.ds(order * 4 + axis, devices, stride=8), :] for axis in range(3)]
        parts.append(jnp.concatenate(columns, axis=1))
    mine = exact_dot(picks_back[...], jnp.concatenate(parts, axis=0))
    for axis in range(3):
        kick[axis] = mine[:, axis * 128 : (axis + 1) * 128]


def on_device(
    tile_mass, tile_frac, tile_cell, tile_level, tile_owner, tile_count, box_owner, force_field
):
    devices = lax.axis_size("boxes")
    levels = box_owner.shape[0]
    tiles, width = tile_mass.shape
    rows = levels * 3 * SIDE
    shape = jax.ShapeDtypeStruct
    vmem = pl.BlockSpec(memory_space=pltpu.VMEM)
    smem = pl.BlockSpec(memory_space=pltpu.SMEM)
    dma = pltpu.SemaphoreType.DMA
    blocks = pltpu.VMEM((devices * 8, width), F32)
    spread_rows = CHUNKS * 2 * SIDE + 16
    density, kick = pl.pallas_call(
        functools.partial(kernel, devices, levels),
        out_shape=(shape((levels * SIDE, CELLS), F32), shape((3, tiles, width), F32)),
        in_specs=[smem] + [pl.BlockSpec(memory_space=pl.ANY)] * 7,
        out_specs=(vmem, vmem),
        scratch_shapes=[
            blocks,
            blocks,
            blocks,
            blocks,
            pltpu.VMEM((1, tiles), jnp.int32),
            pltpu.VMEM(box_owner.shape, jnp.int32),
            pltpu.VMEM((tiles, width), F32),
            pltpu.VMEM((3, tiles, width), F32),
            pltpu.VMEM((tiles, width), jnp.int32),
            pltpu.VMEM((tiles, width), jnp.int32),
            pltpu.VMEM((rows, CELLS), BF16),
            pltpu.VMEM((2 * levels * 7 * devices, devices), BF16),
        ]
        + [pltpu.VMEM((devices // INNER, INNER, 2, 128), F32)] * 2
        + [pltpu.VMEM((devices, 2, 128), F32)] * 2
        + [pltpu.VMEM((devices // INNER, INNER, 1, 128), F32)] * 4
        + [
            pltpu.VMEM((INNER, devices // INNER, 2, 128), F32),
            pltpu.VMEM((2, INNER, devices // INNER, 1, 128), F32),
        ]
        + [
            pltpu.VMEM((rows + 16, WIDE), BF16),
            pltpu.VMEM((WIDE, LANES), BF16),
            pltpu.VMEM((WIDE, LANES), BF16),
            pltpu.VMEM((SHORT + 16, LANES), BF16),
            pltpu.VMEM((SHORT + 16, LANES), BF16),
            pltpu.VMEM((spread_rows, LANES), BF16),
            pltpu.VMEM((spread_rows, LANES), BF16),
            pltpu.VMEM((10 * GROUP, 128), F32),
            pltpu.VMEM((10 * GROUP, 128), F32),
            pltpu.VMEM((GROUP, 128), F32),
            pltpu.VMEM((GROUP, 128), F32),
            pltpu.VMEM((tiles, 2 * devices), BF16),
            pltpu.VMEM((SHORT + 16, 256), F32),
            pltpu.VMEM((WIDE, 128), F32),
            dma,
            dma,
            dma((devices // INNER,)),
            dma,
            dma,
            dma((7,)),
            dma((4, 4)),
        ],
        compiler_params=pltpu.CompilerParams(
            collective_id=0, has_side_effects=True, vmem_limit_bytes=60 << 20
        ),
        name="deposit_and_sample",
    )(
        tile_count,
        tile_owner.reshape(1, tiles),
        box_owner,
        tile_mass,
        jnp.transpose(tile_frac, (1, 0, 2)),
        tile_cell,
        tile_level,
        force_field.reshape(rows, CELLS),
    )
    return (density.reshape(levels, SIDE, CELLS), jnp.transpose(kick, (1, 0, 2)))


def solution(mesh):
    in_specs = (
        P("boxes", None),
        P("boxes", None, None),
        P("boxes", None),
        P("boxes", None),
        P("boxes", None),
        P("boxes"),
        P(),
        P(None, None, "boxes", None),
    )
    out_specs = (P(None, "boxes", None), P("boxes", None, None))
    return jax.shard_map(
        on_device, mesh=mesh, in_specs=in_specs, out_specs=out_specs, check_vma=False
    )
```

```python
import functools

import jax
import jax.numpy as jnp
import numpy as np
from jax import lax
from jax.experimental import pallas as pl
from jax.experimental.pallas import tpu as pltpu
from jax.sharding import PartitionSpec as P

MESH = pl.DeviceIdType.MESH
F32 = jnp.float32
BF16 = jnp.bfloat16
LAT_X = 4
LAT_Z = 4
SIDE = 32
CELLS = SIDE * SIDE
WIDE = CELLS + 128
INNER = 8
GROUP = 2 * INNER
LANES = GROUP * 128
CHUNK = 11
CHUNKS = 3
SHORT = (CHUNK + 1) * SIDE
FORCE_STAGE = 5
MASS_STAGES = (1, 3, 5)

direction_table = np.array(
    [[1, 0, 0], [0, 1, 0], [0, 0, 1], [1, 1, 0], [1, 0, 1], [0, 1, 1], [1, 1, 1]], dtype=np.int32
)


def iota(shape, dim):
    return lax.broadcasted_iota(jnp.int32, shape, dim)


def ones_at(mask, dtype):
    return jnp.where(mask, 1.0, 0.0).astype(dtype)


def exact_dot(picks, values):
    width = values.shape[1]
    high = values.astype(BF16)
    rest = values - high.astype(F32)
    middle = rest.astype(BF16)
    low = (rest - middle.astype(F32)).astype(BF16)
    parts = jnp.concatenate([high, middle, low], axis=1)
    found = jnp.dot(picks, parts, preferred_element_type=F32)
    return (found[:, 0:width] + found[:, width : 2 * width]) + found[:, 2 * width : 3 * width]


def kind_of(value, parts):
    slab = value // 8
    group = slab // 5
    part = slab % 5
    kind = jnp.where(part == 3, 5, part)
    corner = value % 8
    kind = jnp.where(part == 4, jnp.where(corner == 0, 3, jnp.where(corner == 1, 4, 6)), kind)
    return group // parts, kind


def pack_rims(edges, fronts):
    lane = iota((8, 128), 1)
    row = iota((8, 128), 0)
    slabs = []
    for place, front in enumerate(fronts):
        pieces = [front[:, 128 * part : 128 * part + 128] for part in range(8)]
        slabs.append(jnp.concatenate(pieces, axis=0))
        for start in (0, 32, 64):
            total = None
            for part in range(4):
                at = place * SIDE + part * 8
                moved = pltpu.roll(edges[at : at + 8, :], (32 * part - start) % 128, 1)
                total = moved if total is None else jnp.where(lane >= 32 * part, moved, total)
            slabs.append(total)
        last = jnp.broadcast_to(front[:, CELLS:WIDE], (8, 128))
        corners = jnp.where(row == 0, last, pltpu.roll(last, 96, 1))
        slabs.append(jnp.where(row == 2, pltpu.roll(last, 64, 1), corners))
    return jnp.concatenate(slabs, axis=0)


def unpack_rims(values, amount):
    lane = iota((8, 128), 1)
    edges, fronts = [], []
    for place in range(amount):
        at = place * 40
        pieces = [values[at + part : at + part + 1, :] for part in range(8)]
        plane_y, plane_z, line = [values[at + 8 * n : at + 8 * n + 8, :] for n in (1, 2, 3)]
        for part in range(4):
            moved = pltpu.roll(plane_z, (32 - 32 * part) % 128, 1)
            moved = jnp.where(lane < 32, pltpu.roll(plane_y, (-32 * part) % 128, 1), moved)
            moved = jnp.where(lane == 64, pltpu.roll(line, (64 - 32 * part) % 128, 1), moved)
            edges.append(jnp.where(lane <= 64, moved, 0.0))
        corners = values[at + 32 : at + 40, :]
        first = jnp.where(lane < 32, corners, 0.0)[0:1, :]
        second = jnp.where((lane >= 32) & (lane < 64), pltpu.roll(corners, 32, 1), 0.0)[1:2, :]
        third = jnp.where(lane == 64, pltpu.roll(corners, 64, 1), 0.0)[2:3, :]
        fronts.append(jnp.concatenate(pieces + [first + second + third], axis=1))
    return jnp.concatenate(edges, axis=0), fronts


def plane_pick(dtype, flip):
    shape = (128, CELLS) if flip else (CELLS, 128)
    lane = iota(shape, 0 if flip else 1)
    cell = iota(shape, 1 if flip else 0)
    wanted = jnp.where(lane < 32, lane, jnp.where(lane < 64, (lane - 32) * SIDE, -1))
    wanted = jnp.where(lane == 64, 0, wanted)
    return ones_at(cell == wanted, dtype)


def slot_picks(owner_ref, count, by_slot):
    tiles = owner_ref.shape[1]
    across = jnp.broadcast_to(owner_ref[...], (tiles, tiles))
    down = jnp.transpose(across)
    same = across == down
    first, second = iota((tiles, tiles), 0), iota((tiles, tiles), 1)
    if by_slot:
        earlier = jnp.where(same & (first < second), 1.0, 0.0)
        rank = jnp.sum(earlier, axis=0, keepdims=True)
        fits = (across == first) & (second < count)
    else:
        earlier = jnp.where(same & (second < first), 1.0, 0.0)
        rank = jnp.sum(earlier, axis=1, keepdims=True)
        fits = (down == second) & (first < count)
    picks = [jnp.where(fits & (rank == float(order)), 1.0, 0.0) for order in range(2)]
    return jnp.concatenate(picks, axis=0 if by_slot else 1).astype(BF16)


def rim_sources(box_owner, level, devices, sign):
    lat_y = devices // (LAT_X * LAT_Z)
    square = (devices, devices)
    across = jnp.broadcast_to(box_owner[level : level + 1, :], square)
    down = jnp.transpose(across).astype(F32).astype(BF16)
    hot = ones_at(across == iota(square, 0), BF16)
    places = iota(square, 0).astype(F32).astype(BF16)
    box = jnp.dot(hot, places, preferred_element_type=F32).astype(jnp.int32)
    at = [box // (lat_y * LAT_Z), box // LAT_Z % lat_y, box % LAT_Z]
    hots = []
    for step in direction_table:
        near = [
            (at[axis] + (sign * int(step[axis]) + extent)) % extent
            for axis, extent in enumerate((LAT_X, lat_y, LAT_Z))
        ]
        wanted = (near[0] * lat_y + near[1]) * LAT_Z + near[2]
        hots.append(ones_at(wanted == iota(square, 1), BF16))
    owners = jnp.dot(jnp.concatenate(hots, axis=0), down, preferred_element_type=F32)
    return ones_at(owners == iota(owners.shape, 1).astype(F32), BF16)


def choose(hots, values, parts, devices):
    levels = hots.shape[0] // (7 * devices)
    width = values.shape[1]
    level_of, kind = kind_of(iota((1, width), 1) % (128 if parts == 1 else 256), parts)
    total = jnp.zeros((devices, width), F32)
    for level in range(levels):
        at = level * 7 * devices
        found = jnp.dot(hots[at : at + 7 * devices, :], values, preferred_element_type=F32)
        for direction in range(7):
            part = found[direction * devices : (direction + 1) * devices, :]
            total = jnp.where((level_of == level) & (kind == direction), part, total)
    return total


def each(count, act):
    def body(step, carry):
        act(step)
        return carry

    lax.fori_loop(1, count, body, 0)


def block_rows(device):
    return pl.ds(pl.multiple_of(device * 8, 8), 8)


def block_copy(source, target, send, recv, peer, me):
    return pltpu.make_async_remote_copy(
        src_ref=source.at[block_rows(peer)],
        dst_ref=target.at[block_rows(me)],
        send_sem=send,
        recv_sem=recv,
        device_id=(peer,),
        device_id_type=MESH,
    )


def all_blocks(source, target, send, recv, devices, me):
    rows = (devices - 1) * 8
    return pltpu.make_async_remote_copy(
        src_ref=source.at[pl.ds(0, rows)],
        dst_ref=target.at[pl.ds(0, rows)],
        send_sem=send,
        recv_sem=recv,
        device_id=(lax.rem(me + 1, devices),),
        device_id_type=MESH,
    )


def rim_hops(source, middle, target, sems, devices, me):
    rows = devices // INNER
    row, place = me // INNER, lax.rem(me, INNER)

    def first(step):
        other = lax.rem(place + step, INNER)
        return pltpu.make_async_remote_copy(
            src_ref=source.at[:, other],
            dst_ref=middle.at[place],
            send_sem=sems.at[0],
            recv_sem=sems.at[1],
            device_id=(row * INNER + other,),
            device_id_type=MESH,
        )

    def second(step):
        other = lax.rem(row + step, rows)
        return pltpu.make_async_remote_copy(
            src_ref=middle.at[:, other],
            dst_ref=target.at[row],
            send_sem=sems.at[2],
            recv_sem=sems.at[3],
            device_id=(other * INNER + place,),
            device_id_type=MESH,
        )

    def start():
        each(INNER, lambda step: first(step).start())
        middle[place] = source[:, place]

    def forward():
        pltpu.make_async_remote_copy(
            src_ref=middle.at[pl.ds(0, INNER - 1)],
            dst_ref=middle.at[pl.ds(0, INNER - 1)],
            send_sem=sems.at[0],
            recv_sem=sems.at[1],
            device_id=(row * INNER + lax.rem(place + 1, INNER),),
            device_id_type=MESH,
        ).wait()
        each(rows, lambda step: second(step).start())
        target[row] = middle[:, row]

    def finish():
        pltpu.make_async_remote_copy(
            src_ref=target.at[pl.ds(0, rows - 1)],
            dst_ref=target.at[pl.ds(0, rows - 1)],
            send_sem=sems.at[2],
            recv_sem=sems.at[3],
            device_id=(lax.rem(row + 1, rows) * INNER + place,),
            device_id_type=MESH,
        ).wait()

    return start, forward, finish


def rim_copy(source, target, sems, peer, me):
    return pltpu.make_async_remote_copy(
        src_ref=source.at[peer],
        dst_ref=target.at[me],
        send_sem=sems.at[0],
        recv_sem=sems.at[1],
        device_id=(peer,),
        device_id_type=MESH,
    )


def all_rims(source, target, sems, devices, me):
    return pltpu.make_async_remote_copy(
        src_ref=source.at[pl.ds(0, devices - 1)],
        dst_ref=target.at[pl.ds(0, devices - 1)],
        send_sem=sems.at[0],
        recv_sem=sems.at[1],
        device_id=(lax.rem(me + 1, devices),),
        device_id_type=MESH,
    )


def hat(coord, rows):
    ids = iota((rows, coord.shape[1]), 0).astype(F32)
    return jnp.maximum(0.0, 1.0 - jnp.abs(coord - ids))


def group_fields(inbox, first):
    return [inbox[pl.ds(first + field, GROUP, stride=4), :] for field in range(4)]


def flat(ref, first, stride):
    return jnp.concatenate([ref[pl.ds(first + t * stride, 1), :] for t in range(GROUP)], axis=1)


def end_hat(coord):
    return jnp.maximum(0.0, 1.0 - jnp.abs(coord - float(SIDE)))


def keep(rows, values):
    for place, value in enumerate(values):
        rows[place * GROUP : (place + 1) * GROUP, :] = value
    return [flat(rows, place * GROUP, 1) for place in range(len(values))]


def fill_deposit(inbox, first, rows, short, weighted):
    mass, x, y, z = group_fields(inbox, first)
    chunk = jnp.where(y >= 2.0 * CHUNK, 2.0, jnp.where(y >= CHUNK, 1.0, 0.0))
    row_of = 2.0 * chunk + jnp.where(mass < 0.0, 1.0, 0.0)
    size = jnp.abs(mass)
    owns = [jnp.where(row_of == float(place), size, 0.0) for place in range(CHUNKS * 2)]
    rest = [y - chunk * CHUNK, end_hat(z), row_of, size * end_hat(x)]
    *owns, near_y, end_z, row_of, end_x = keep(rows, owns + rest)
    hat_x = hat(flat(inbox, first + 1, 4), SIDE)
    hat_y = hat(near_y, 16)
    hat_z = hat(flat(inbox, first + 3, 4), SIDE)
    for row in range(CHUNK + 1):
        short[row * SIDE : (row + 1) * SIDE, :] = (hat_y[row : row + 1, :] * hat_z).astype(BF16)
    short[SHORT : SHORT + 16, :] = (hat_y * end_z).astype(BF16)
    for place, own in enumerate(owns):
        weighted[place * SIDE : (place + 1) * SIDE, :] = (own * hat_x).astype(BF16)
    ends = jnp.where(iota((16, LANES), 0).astype(F32) == row_of, end_x, 0.0)
    at = CHUNKS * 2 * SIDE
    weighted[at : at + 16, :] = ends.astype(BF16)


def add_deposit(short, weighted, total):
    product = lax.dot_general(
        short[...], weighted[...], (((1,), (1,)), ((), ())), preferred_element_type=F32
    )
    total[:, 0 : product.shape[1]] += product


def fill_cross(inbox, first, rows, cross):
    _, _, y, z = group_fields(inbox, first)
    end_y, end_z = end_hat(y), end_hat(z)
    end_y, end_z, end_both = keep(rows, [end_y, end_z, end_y * end_z])
    hat_y = hat(flat(inbox, first + 2, 4), SIDE)
    hat_z = hat(flat(inbox, first + 3, 4), SIDE)
    for row in range(SIDE):
        cross[row * SIDE : (row + 1) * SIDE, :] = (hat_y[row : row + 1, :] * hat_z).astype(BF16)
    cross[CELLS : CELLS + 32, :] = (end_y * hat_z).astype(BF16)
    cross[CELLS + 32 : CELLS + 64, :] = (hat_y * end_z).astype(BF16)
    last = jnp.where(iota((16, LANES), 0) == 0, end_both, 0.0)
    cross[CELLS + 64 : CELLS + 80, :] = last.astype(BF16)


def sample(inbox, first, rows, table, cross, kicks):
    mass, x, _, _ = group_fields(inbox, first)
    (end_x,) = keep(rows, [end_hat(x)])
    hat_x = hat(flat(inbox, first + 1, 4), SIDE)
    upper_level = flat(inbox, first, 4) < 0.0
    amount = table.shape[0] - 16
    depth = amount // 2
    sampled = jnp.dot(table[...], cross[...], preferred_element_type=F32)
    for axis in range(3):
        at = axis * SIDE
        picked = jnp.where(
            upper_level, sampled[depth + at : depth + at + SIDE, :], sampled[at : at + SIDE, :]
        )
        at = amount + axis
        far = jnp.where(upper_level, sampled[at + 3 : at + 4, :], sampled[at : at + 1, :])
        value = jnp.sum(hat_x * picked, axis=0, keepdims=True) + end_x * far
        for t in range(GROUP):
            kicks[pl.ds(first + (t * 4 + axis), 1), :] = value[:, t * 128 : (t + 1) * 128]


def spread_deposit(total, wide):
    wide[...] = jnp.zeros_like(wide)
    first, second = total[:, 0:128], total[:, 128:256]
    low = iota(first.shape, 1) < 2 * SIDE
    for place in range(CHUNKS):
        main = [first, pltpu.roll(first, 64, 1), second][place]
        ends = second if place == 0 else pltpu.roll(second, 128 - 2 * place, 1)
        both = jnp.where(low, main, ends)
        at = place * CHUNK * SIDE
        wide[at : at + SHORT, :] += both[0:SHORT, :]
        at = CELLS + SIDE + place * CHUNK
        wide[at : at + CHUNK + 1, :] += both[SHORT : SHORT + CHUNK + 1, :]


def kernel(
    devices,
    levels,
    count_ref,
    owner_in,
    box_in,
    mass_in,
    frac_in,
    cell_in,
    level_in,
    force_in,
    density,
    kick,
    outbox,
    inbox,
    kicks,
    returned,
    owner_ref,
    box_owner,
    mass_ref,
    frac_ref,
    cell_ref,
    level_ref,
    force_ref,
    hots,
    force_out,
    force_spread,
    force_next,
    force_last,
    mass_out,
    mass_spread,
    mass_next,
    mass_last,
    force_middle,
    mass_middle,
    table,
    cross_a,
    cross_b,
    short_a,
    short_b,
    weighted_a,
    weighted_b,
    rows_a,
    rows_b,
    rows_c,
    rows_d,
    picks_back,
    total,
    wide,
    own_sem,
    tile_send,
    tile_recv,
    kick_send,
    kick_recv,
    load_sem,
    rim_sems,
):
    me = lax.axis_index("boxes")
    depth = 3 * SIDE
    rows = levels * depth
    groups = devices // INNER
    my_row = me // INNER
    pairs = groups // 2

    loads = [
        pltpu.make_async_copy(source, target, load_sem.at[place])
        for place, (source, target) in enumerate(
            [
                (owner_in, owner_ref),
                (mass_in, mass_ref),
                (frac_in, frac_ref),
                (cell_in, cell_ref),
                (level_in, level_ref),
                (force_in, force_ref),
                (box_in, box_owner),
            ]
        )
    ]
    for load in loads:
        load.start()
    barrier = pltpu.get_barrier_semaphore()
    each(
        devices,
        lambda step: pl.semaphore_signal(
            barrier, inc=1, device_id=(lax.rem(me + step, devices),), device_id_type=MESH
        ),
    )

    loads[0].wait()
    picks = slot_picks(owner_ref, count_ref[0], True)
    for load in loads[1:5]:
        load.wait()
    cell = cell_ref[...]
    digits = [cell // CELLS, cell // SIDE % SIDE, cell % SIDE]
    fields = [jnp.where(level_ref[...] == 0, mass_ref[...], -mass_ref[...])]
    for axis in range(3):
        fields.append(digits[axis].astype(F32) + frac_ref[axis])
    packed = exact_dot(picks, jnp.concatenate(fields, axis=1))
    for order in range(2):
        for field in range(4):
            part = packed[order * devices : (order + 1) * devices, field * 128 : field * 128 + 128]
            outbox[pl.ds(order * 4 + field, devices, stride=8), :] = part

    loads[5].wait()
    loads[6].wait()
    force = force_ref[...]
    edges = jnp.dot(force, plane_pick(BF16, False), preferred_element_type=F32)
    fronts = []
    for place in range(levels * 3):
        at = place * SIDE
        front = force_ref[at : at + 16, :].astype(F32)[0:1, :]
        fronts.append(jnp.concatenate([front, edges[at : at + 1, :]], axis=1))
    values = pack_rims(edges, fronts)
    values = jnp.concatenate([values, jnp.zeros((256 - values.shape[0], 128), F32)], axis=0)
    for half in range(2):
        block = jnp.transpose(values[half * 128 : half * 128 + 128, :])
        force_out[:, :, half, :] = block.reshape(devices // INNER, INNER, 128)
    pl.semaphore_wait(barrier, devices - 1)

    force_hops = rim_hops(force_out, force_middle, force_spread, rim_sems.at[0], devices, me)
    mass_hops = [
        rim_hops(mass_out, mass_middle.at[0], mass_spread, rim_sems.at[2], devices, me),
        rim_hops(mass_next, mass_middle.at[1], mass_last, rim_sems.at[3], devices, me),
    ]

    def tile_copy(hop, peer):
        return block_copy(outbox, inbox, tile_send, tile_recv.at[hop], peer, me)

    def send_tiles(hop):
        target = lax.rem(my_row + hop, groups) * INNER
        each(INNER, lambda step: tile_copy(hop, target + lax.rem(me + step, INNER)).start())

        @pl.when(hop > 0)
        def _():
            tile_copy(hop, target + lax.rem(me, INNER)).start()

    force_hops[0]()
    send_tiles(0)
    each(groups, send_tiles)
    own = pltpu.make_async_copy(outbox.at[block_rows(me)], inbox.at[block_rows(me)], own_sem)
    own.start()
    force_hops[1]()

    def find_sources(way, sign):
        for level in range(levels):
            first = (way * levels + level) * 7 * devices
            hots[pl.ds(first, 7 * devices), :] = rim_sources(box_owner, level, devices, sign)

    find_sources(0, 1)
    table[0:rows, 0:CELLS] = force
    blank = jnp.zeros((WIDE - CELLS - 80, LANES), BF16)
    cross_a[CELLS + 80 : WIDE, :] = blank
    cross_b[CELLS + 80 : WIDE, :] = blank
    total[...] = jnp.zeros_like(total)
    kicks[...] = jnp.zeros_like(kicks)

    def force_relay():
        force_hops[2]()
        values = jnp.concatenate(
            [force_spread[:, :, half, :].reshape(devices, 128) for half in range(2)], axis=1
        )
        chosen = choose(hots[0 : levels * 7 * devices, :], values.astype(BF16), 3, devices)
        for half in range(2):
            force_next[:, half, :] = chosen[:, half * 128 : half * 128 + 128]
        each(
            devices,
            lambda step: rim_copy(
                force_next, force_last, rim_sems.at[1], lax.rem(me + step, devices), me
            ).start(),
        )
        force_last[me] = force_next[me]

    def mass_relay():
        mass_hops[0][2]()
        values = mass_spread[:, :, 0, :].reshape(devices, 128)
        high = values.astype(BF16)
        rest = (values - high.astype(F32)).astype(BF16)
        way = hots[levels * 7 * devices : 2 * levels * 7 * devices, :]
        chosen = choose(way, jnp.concatenate([high, rest], axis=1), 1, devices)
        chosen = chosen[:, 0:128] + chosen[:, 128:256]
        mass_next[:, :, 0, :] = chosen.reshape(devices // INNER, INNER, 128)
        mass_hops[1][0]()

    def stages(pair, at, acts):
        for place, act in zip(at, acts):
            pl.when(pair == place)(act)

    def await_group(hop):
        amount = devices // groups * 8
        if isinstance(hop, int) and hop == 0:
            own.wait()
            amount -= 8
        pltpu.make_async_remote_copy(
            src_ref=outbox.at[pl.ds(0, amount)],
            dst_ref=inbox.at[pl.ds(0, amount)],
            send_sem=tile_send,
            recv_sem=tile_recv.at[hop],
            device_id=(lax.rem(me + 1, devices),),
            device_id_type=MESH,
        ).wait_recv()

    def first_of(hop):
        return pl.multiple_of(lax.rem(my_row + groups - hop, groups) * (INNER * 8), 8)

    def fill_a(hop):
        fill_deposit(inbox, first_of(hop), rows_a, short_a, weighted_a)

    def fill_b(hop):
        fill_deposit(inbox, first_of(hop), rows_b, short_b, weighted_b)

    await_group(0)
    fill_a(0)

    def deposit_pair(pair, carry):
        pl.when(pair == FORCE_STAGE)(force_relay)
        await_group(2 * pair + 1)
        await_group(2 * pair + 2)
        fill_b(2 * pair + 1)
        add_deposit(short_a, weighted_a, total)
        fill_a(2 * pair + 2)
        add_deposit(short_b, weighted_b, total)
        return carry

    lax.fori_loop(0, pairs - 1, deposit_pair, 0)
    await_group(groups - 1)
    fill_b(groups - 1)
    add_deposit(short_a, weighted_a, total)
    add_deposit(short_b, weighted_b, total)

    spread_deposit(total, wide)
    flipped = jnp.transpose(wide[...])
    density[...] = flipped[0 : levels * SIDE, 0:CELLS]
    beyond = flipped[levels * SIDE : levels * SIDE + levels, :]
    values = pack_rims(
        flipped[0 : levels * SIDE, CELLS:WIDE],
        [beyond[level : level + 1, :] for level in range(levels)],
    )
    values = jnp.concatenate([values, jnp.zeros((128 - values.shape[0], 128), F32)], axis=0)
    mass_out[:, :, 0, :] = jnp.transpose(values).reshape(devices // INNER, INNER, 128)
    mass_hops[0][0]()

    def kick_copy(peer):
        return block_copy(kicks, returned, kick_send, kick_recv, peer, me)

    def send_kicks(hop):
        target = lax.rem(my_row + groups - hop, groups) * INNER
        for place in range(INNER):
            kick_copy(target + place).start()

    def cross_a_of(hop):
        fill_cross(inbox, first_of(hop), rows_a, cross_a)

    def cross_b_of(hop):
        fill_cross(inbox, first_of(hop), rows_b, cross_b)

    def sample_a_of(hop):
        sample(inbox, first_of(hop), rows_c, table, cross_a, kicks)

    def sample_b_of(hop):
        sample(inbox, first_of(hop), rows_d, table, cross_b, kicks)

    cross_a_of(1)

    find_sources(1, -1)
    picks_back[...] = slot_picks(owner_ref, count_ref[0], False)
    all_rims(force_next, force_last, rim_sems.at[1], devices, me).wait()
    values = jnp.concatenate(
        [jnp.transpose(force_last[:, half, :]) for half in range(2)], axis=0
    )
    edges, fronts = unpack_rims(values, levels * 3)
    table[0:rows, CELLS:WIDE] = edges.astype(BF16)
    fronts.append(jnp.zeros((16 - len(fronts), WIDE), F32))
    table[rows : rows + 16, :] = jnp.concatenate(fronts, axis=0).astype(BF16)

    def sample_pair(pair, carry):
        stages(pair, MASS_STAGES, (mass_hops[0][1], mass_relay, mass_hops[1][1]))
        cross_b_of(2 * pair + 2)
        sample_a_of(2 * pair + 1)
        cross_a_of(2 * pair + 3)
        sample_b_of(2 * pair + 2)
        send_kicks(2 * pair + 1)
        send_kicks(2 * pair + 2)
        return carry

    lax.fori_loop(0, pairs - 1, sample_pair, 0)
    cross_b_of(0)
    sample_a_of(groups - 1)
    send_kicks(groups - 1)
    sample_b_of(0)
    each(INNER, lambda step: kick_copy(my_row * INNER + lax.rem(me + step, INNER)).start())
    kept = pltpu.make_async_copy(kicks.at[block_rows(me)], returned.at[block_rows(me)], own_sem)
    kept.start()

    mass_hops[1][2]()
    values = jnp.transpose(mass_last[:, :, 0, :].reshape(devices, 128))
    edges, fronts = unpack_rims(values, levels)
    first_row = iota((SIDE, 1), 0) == 0
    low = [
        edges[level * SIDE : (level + 1) * SIDE, :]
        + jnp.where(first_row, fronts[level][:, CELLS:WIDE], 0.0)
        for level in range(levels)
    ]
    low = jnp.concatenate(low, axis=0)
    high = low.astype(BF16)
    pair = jnp.concatenate([high, (low - high.astype(F32)).astype(BF16)], axis=0)
    added = jnp.dot(pair, plane_pick(BF16, True), preferred_element_type=F32)
    added = added[0 : levels * SIDE, :] + added[levels * SIDE : 2 * levels * SIDE, :]
    for level in range(levels):
        at = slice(level * SIDE, (level + 1) * SIDE)
        density[at, :] += added[at, :] + jnp.where(first_row, fronts[level][:, 0:CELLS], 0.0)

    all_blocks(outbox, inbox, tile_send, tile_recv.at[0], devices, me).wait_send()
    kept.wait()
    all_blocks(kicks, returned, kick_send, kick_recv, devices, me).wait()
    parts = []
    for order in range(2):
        columns = [returned[pl.ds(order * 4 + axis, devices, stride=8), :] for axis in range(3)]
        parts.append(jnp.concatenate(columns, axis=1))
    mine = exact_dot(picks_back[...], jnp.concatenate(parts, axis=0))
    for axis in range(3):
        kick[axis] = mine[:, axis * 128 : (axis + 1) * 128]


def on_device(
    tile_mass, tile_frac, tile_cell, tile_level, tile_owner, tile_count, box_owner, force_field
):
    devices = lax.axis_size("boxes")
    levels = box_owner.shape[0]
    tiles, width = tile_mass.shape
    rows = levels * 3 * SIDE
    shape = jax.ShapeDtypeStruct
    vmem = pl.BlockSpec(memory_space=pltpu.VMEM)
    smem = pl.BlockSpec(memory_space=pltpu.SMEM)
    dma = pltpu.SemaphoreType.DMA
    blocks = pltpu.VMEM((devices * 8, width), F32)
    spread_rows = CHUNKS * 2 * SIDE + 16
    density, kick = pl.pallas_call(
        functools.partial(kernel, devices, levels),
        out_shape=(shape((levels * SIDE, CELLS), F32), shape((3, tiles, width), F32)),
        in_specs=[smem] + [pl.BlockSpec(memory_space=pl.ANY)] * 7,
        out_specs=(vmem, vmem),
        scratch_shapes=[
            blocks,
            blocks,
            blocks,
            blocks,
            pltpu.VMEM((1, tiles), jnp.int32),
            pltpu.VMEM(box_owner.shape, jnp.int32),
            pltpu.VMEM((tiles, width), F32),
            pltpu.VMEM((3, tiles, width), F32),
            pltpu.VMEM((tiles, width), jnp.int32),
            pltpu.VMEM((tiles, width), jnp.int32),
            pltpu.VMEM((rows, CELLS), BF16),
            pltpu.VMEM((2 * levels * 7 * devices, devices), BF16),
        ]
        + [pltpu.VMEM((devices // INNER, INNER, 2, 128), F32)] * 2
        + [pltpu.VMEM((devices, 2, 128), F32)] * 2
        + [pltpu.VMEM((devices // INNER, INNER, 1, 128), F32)] * 4
        + [
            pltpu.VMEM((INNER, devices // INNER, 2, 128), F32),
            pltpu.VMEM((2, INNER, devices // INNER, 1, 128), F32),
        ]
        + [
            pltpu.VMEM((rows + 16, WIDE), BF16),
            pltpu.VMEM((WIDE, LANES), BF16),
            pltpu.VMEM((WIDE, LANES), BF16),
            pltpu.VMEM((SHORT + 16, LANES), BF16),
            pltpu.VMEM((SHORT + 16, LANES), BF16),
            pltpu.VMEM((spread_rows, LANES), BF16),
            pltpu.VMEM((spread_rows, LANES), BF16),
            pltpu.VMEM((10 * GROUP, 128), F32),
            pltpu.VMEM((10 * GROUP, 128), F32),
            pltpu.VMEM((GROUP, 128), F32),
            pltpu.VMEM((GROUP, 128), F32),
            pltpu.VMEM((tiles, 2 * devices), BF16),
            pltpu.VMEM((SHORT + 16, 256), F32),
            pltpu.VMEM((WIDE, 128), F32),
            dma,
            dma,
            dma((devices // INNER,)),
            dma,
            dma,
            dma((7,)),
            dma((4, 4)),
        ],
        compiler_params=pltpu.CompilerParams(
            collective_id=0, has_side_effects=True, vmem_limit_bytes=60 << 20
        ),
        name="deposit_and_sample",
    )(
        tile_count,
        tile_owner.reshape(1, tiles),
        box_owner,
        tile_mass,
        jnp.transpose(tile_frac, (1, 0, 2)),
        tile_cell,
        tile_level,
        force_field.reshape(rows, CELLS),
    )
    return (density.reshape(levels, SIDE, CELLS), jnp.transpose(kick, (1, 0, 2)))


def solution(mesh):
    in_specs = (
        P("boxes", None),
        P("boxes", None, None),
        P("boxes", None),
        P("boxes", None),
        P("boxes", None),
        P("boxes"),
        P(),
        P(None, None, "boxes", None),
    )
    out_specs = (P(None, "boxes", None), P("boxes", None, None))
    return jax.shard_map(
        on_device, mesh=mesh, in_specs=in_specs, out_specs=out_specs, check_vma=False
    )
```
